256 devices in a mesh: grp: 8 (over x_hi, y), col: 32 (over z, x_lo, core).
Axes of the slice: x: 4 (x_hi: 2, x_lo: 2; x = x_hi * 2 + x_lo), y: 4, z: 8, core: 2. Of those that a mesh axis runs over, the one named last changes fastest.
Arguments:
- image_learn: bfloat16 [16384, 1152], P(('grp', 'col')), may hold values from -6 to 6
- image_refer: bfloat16 [16384, 1152], P(('grp', 'col')), may hold values from -6 to 6
- text_learn: bfloat16 [32, 1536, 1152], P('col', 'grp'), may hold values from -6 to 6
- text_refer: bfloat16 [32, 1536, 1152], P('col', 'grp'), may hold values from -6 to 6
- image_scale_learn: float32 [16384], P('grp'), may hold values from 0.03432945 to 0.102988355
- image_scale_refer: float32 [16384], P('grp'), may hold values from 0.03432945 to 0.102988355
- text_scale_learn: float32 [49152], P('col'), may hold values from 0.03432945 to 0.102988355
- text_scale_refer: float32 [49152], P('col'), may hold values from 0.03432945 to 0.102988355
- pair_index: int32 [16384], P('grp'), may hold values from 0 to 49151
Outputs:
- row_sum: float32 [16384], P(('grp', 'col'))
- col_sum: float32 [49152], P('col')
The draws below stay inside these ranges and needn't reach their ends.
All inputs are finite; a program needn't handle non-finite values.
Results may differ from the reference program's by a relative error of at most 0.0003.
Values may be sent and summed in bfloat16 or wider, within the bound.
A program may use at most 128 MiB of HBM per device.

```python
import math
import jax
import jax.numpy as jnp
from jax import lax

E = 1152
COL_BLK = 1536
B_IMG = 16384
B_TXT = 49152
N_COL = 32


def with_ends(values, rng, least, largest):
    index_at = [jax.random.randint(jax.random.fold_in(rng, axis), (), 0, length) for axis, length in enumerate(values.shape)]
    main_axis = values.shape.index(max(values.shape))
    neighbour = index_at[:main_axis] + [(index_at[main_axis] + 1) % values.shape[main_axis]] + index_at[main_axis + 1:]
    return values.at[tuple(index_at)].set(least).at[tuple(neighbour)].set(largest)


def block_levels(key, shape, cuts, smallest, high):
    def one(position, shards_of):
        steps = jax.random.uniform(jax.random.fold_in(jax.random.fold_in(key, 6), position), (shards_of,), jnp.float32, smallest / len(cuts), high / len(cuts))
        return jnp.repeat(jnp.exp(steps), shape[position] // shards_of).reshape((-1,) + (1,) * (len(shape) - position - 1))

    factor_of = one(*cuts[0])
    for cut in cuts[1:]:
        factor_of = factor_of * one(*cut)
    return factor_of


def normal_values(rng, dims, scale, reach, split=(), held_as=jnp.bfloat16):
    values = jax.random.normal(rng, dims, jnp.float32) * scale
    if len(split) > 0:
        values = block_levels(rng, dims, split, -0.22, 0.18) * values
    return jnp.clip(values, min=-reach, max=reach).astype(held_as)


def setup_inputs(seed: int = 0) -> dict:
    arg_keys = jax.random.split(jax.random.key(seed), 10)
    image_learn = normal_values(arg_keys[0], (B_IMG, E), 1.0, 6.0, ((0, 256),))
    image_refer = normal_values(arg_keys[1], (B_IMG, E), 1.0, 6.0, ((0, 256),))
    text_learn = normal_values(arg_keys[2], (N_COL, COL_BLK, E), 1.0, 6.0, ((0, 32), (1, 8)))
    text_refer = normal_values(arg_keys[3], (N_COL, COL_BLK, E), 1.0, 6.0, ((0, 32), (1, 8)))
    image_scale_learn = jnp.clip(jnp.exp(math.log(0.102988355) - 1.0986123 * jax.random.uniform(arg_keys[4], (B_IMG,), jnp.float32) ** block_levels(arg_keys[4], (B_IMG,), ((0, 8),), -0.2, 0.2)), 0.03432945, 0.102988355)
    image_scale_refer = jnp.clip(jnp.exp(math.log(0.102988355) - 1.0986123 * jax.random.uniform(arg_keys[5], (B_IMG,), jnp.float32) ** block_levels(arg_keys[5], (B_IMG,), ((0, 8),), -0.2, 0.2)), 0.03432945, 0.102988355)
    text_scale_learn = jnp.clip(jnp.exp(math.log(0.102988355) - 1.0986123 * jax.random.uniform(arg_keys[6], (B_TXT,), jnp.float32) ** block_levels(arg_keys[6], (B_TXT,), ((0, 32),), -0.2, 0.2)), 0.03432945, 0.102988355)
    text_scale_refer = jnp.clip(jnp.exp(math.log(0.102988355) - 1.0986123 * jax.random.uniform(arg_keys[7], (B_TXT,), jnp.float32) ** block_levels(arg_keys[7], (B_TXT,), ((0, 32),), -0.2, 0.2)), 0.03432945, 0.102988355)
    pair_index = with_ends(jax.random.randint(arg_keys[8], (B_IMG,), 0, B_TXT), jax.random.fold_in(arg_keys[8], 1), 0, B_TXT - 1).astype(jnp.int32)
    return dict(image_learn=image_learn, image_refer=image_refer, text_learn=text_learn, text_refer=text_refer, image_scale_learn=image_scale_learn, image_scale_refer=image_scale_refer, text_scale_learn=text_scale_learn, text_scale_refer=text_scale_refer, pair_index=pair_index)


def pair_score(learn_sim, refer_sim, positive, offset):
    sign = jnp.where(positive, jnp.float32(1.0), jnp.float32(-1.0))
    first = jax.nn.softplus(-sign * ((4.0 * learn_sim + 1.0) - offset))
    second = jax.nn.softplus(-sign * ((6.0 * refer_sim - 1.0) - offset))
    return first - second


def reference(image_learn, image_refer, text_learn, text_refer, image_scale_learn, image_scale_refer, text_scale_learn, text_scale_refer, pair_index):
    block = min(512, B_IMG)
    count = B_IMG // block
    offset = math.log(B_TXT)
    columns = jnp.arange(B_TXT, dtype=jnp.int32)
    flat_learn = text_learn.reshape(B_TXT, E)
    flat_refer = text_refer.reshape(B_TXT, E)
    items = (image_learn.reshape(count, block, E), image_refer.reshape(count, block, E),
             image_scale_learn.reshape(count, block), image_scale_refer.reshape(count, block),
             pair_index.reshape(count, block))

    def step(carry, item):
        rows_learn, rows_refer, scale_learn, scale_refer, pairs = item
        learn_sim = jnp.dot(rows_learn, flat_learn.T, preferred_element_type=jnp.float32) * scale_learn[:, None] * text_scale_learn[None, :]
        refer_sim = jnp.dot(rows_refer, flat_refer.T, preferred_element_type=jnp.float32) * scale_refer[:, None] * text_scale_refer[None, :]
        learned = pair_score(learn_sim, refer_sim, pairs[:, None] == columns[None, :], offset)
        return carry + jnp.sum(learned, axis=0), jnp.sum(learned, axis=1)

    col_total, row_total = lax.scan(step, jnp.zeros((B_TXT,), jnp.float32), items)
    return row_total.reshape(B_IMG), col_total
```

```python
import functools
import math

import jax
import jax.numpy as jnp
from jax import lax
from jax.experimental import pallas as pl
from jax.experimental.pallas import tpu as pltpu
from jax.sharding import PartitionSpec as P

F32 = jnp.float32
LOG2E = 1.0 / math.log(2.0)
LN2 = math.log(2.0)
SERIES = tuple(2.0 * LOG2E * c for c in (0.99999984, 0.33337989, 0.1979503, 0.17111227))

E = 1152
HALF = 96
CHUNK = 4 * HALF
SLOT = 256
SLOT_Z = (0, 1, -1, 2, -2, 3, -3, 4)
STEPS = 32


def wrap(value, size):
    return lax.rem(value + size, size)


def score(dot_learn, dot_refer, a_learn, a_refer, b_learn, b_refer, paired, c_learn, c_refer):
    u = dot_learn * a_learn * b_learn + c_learn
    w = dot_refer * a_refer * b_refer + c_refer
    p = jnp.exp2(-jnp.abs(u))
    q = jnp.exp2(-jnp.abs(w))
    z = (p - q) * pl.reciprocal((p + q) + 2.0, approx=True)
    s = z * z
    poly = s * SERIES[3] + SERIES[2]
    poly = poly * s + SERIES[1]
    poly = poly * s + SERIES[0]
    d = (jnp.maximum(u, 0.0) - jnp.maximum(w, 0.0)) + z * poly
    return d - jnp.where(paired, u - w, 0.0)


def kernel(
    c_learn,
    c_refer,
    img_l,
    img_r,
    txt_l,
    txt_r,
    isc_l,
    isc_r,
    tsc_l,
    tsc_r,
    pair,
    row_out,
    col_out,
    tb,
    ib,
    isc,
    ipr,
    tsc,
    bc,
    tcol,
    irow,
    iprow,
    base,
    rs,
    cs,
    dl0,
    dr0,
    dl1,
    dr1,
    row_part,
    row_recv,
    col_part,
    col_recv,
    local_sem,
    send_sem,
    recv_sem,
    row_send,
    row_got,
    col_send,
    col_got,
    ready,
):
    grp, col = lax.axis_index("grp"), lax.axis_index("col")
    x = lax.div(grp, 4) * 2 + lax.rem(lax.div(col, 2), 2)
    y = lax.rem(grp, 4)
    z = lax.div(col, 4)
    core = lax.rem(col, 2)
    x_odd, y_odd = lax.rem(x, 2), lax.rem(y, 2)
    x_pair, y_pair = x + 1 - 2 * x_odd, y + 1 - 2 * y_odd
    x_diag, y_diag = wrap(x - 1 + 2 * x_odd, 4), wrap(y - 1 + 2 * y_odd, 4)

    def device(dx=0, dy=0, dz=0, at_x=None, at_y=None, at_core=None):
        px = wrap(x + dx, 4) if at_x is None else at_x
        py = wrap(y + dy, 4) if at_y is None else at_y
        pz = wrap(z + dz, 8)
        pc = core if at_core is None else at_core
        return lax.div(px, 2) * 4 + py, (pz * 2 + lax.rem(px, 2)) * 2 + pc

    other_core = device(at_core=1 - core)
    diag = device(at_x=x_diag, at_y=y_diag)
    to_x_pair, to_y_pair = device(at_x=x_pair), device(at_y=y_pair)
    up_x, dn_x = device(dx=1), device(dx=-1)
    up_y, dn_y = device(dy=1), device(dy=-1)
    up_z, dn_z = device(dz=1), device(dz=-1)

    messages = {}

    def message(name, src, dst, to):
        messages[name] = (len(messages), src, dst, to)

    def text(piece, part=None):
        off, rows = (piece * HALF, HALF) if part is None else (piece * HALF + part * (HALF // 2), HALF // 2)
        return tb.at[:, pl.ds(off, rows), :]

    def image(slot, lane, part=None):
        rows = 64 if part is None else 32
        off = slot * SLOT + lane * 128 + core * 64 + (0 if part is None else part * 32)
        return ib.at[:, pl.ds(pl.multiple_of(off, 32), rows), :]

    message("t1p", text(0), text(2), to_x_pair)
    message("t2p", text(1), text(3), to_y_pair)
    message("ip", image(0, 0), image(0, 1), diag)
    message("tsc", tsc.at[0], tsc.at[1], to_x_pair)
    message("isc", isc.at[0], isc.at[1], diag)
    message("ipr", ipr.at[0], ipr.at[1], diag)
    for name, first, up, dn in (("t1", 0, up_y, dn_y), ("t2", 1, up_x, dn_x)):
        o = 4 + 2 * first
        message(name + "o-", text(first), text(o + 1), up)
        message(name + "o+", text(first), text(o), dn)
        message(name + "q-", text(2 + first), text(o + 5), up)
        message(name + "q+", text(2 + first), text(o + 4), dn)
        far = 12 + 2 * first
        message(name + "o2+", text(o, 0), text(far, 0), dn)
        message(name + "o2-", text(o + 1, 1), text(far, 1), up)
        message(name + "q2+", text(o + 4, 0), text(far + 1, 0), dn)
        message(name + "q2-", text(o + 5, 1), text(far + 1, 1), up)
    for lane, mark in ((0, "o"), (1, "q")):
        for k in (1, 2, 3):
            came_p, came_m = (0, 0) if k == 1 else (2 * k - 3, 2 * k - 2)
            message(f"i{mark}{k}+", image(came_p, lane), image(2 * k - 1, lane), dn_z)
            message(f"i{mark}{k}-", image(came_m, lane), image(2 * k, lane), up_z)
        message(f"i{mark}4+", image(5, lane, 0), image(7, lane, 0), dn_z)
        message(f"i{mark}4-", image(6, lane, 1), image(7, lane, 1), up_z)
        for slot in range(8):
            message(f"s{mark}{slot}", image(slot, lane), image(slot, lane), other_core)

    def copy(name):
        number, src, dst, to = messages[name]
        return pltpu.make_async_remote_copy(
            src_ref=src,
            dst_ref=dst,
            send_sem=send_sem.at[number],
            recv_sem=recv_sem.at[number],
            device_id=to,
            device_id_type=pl.DeviceIdType.MESH,
        )

    def start(*names):
        for name in names:
            copy(name).start()

    def got(*names):
        for name in names:
            if name[0] == "s":
                number, _, _, to = messages[name]
                slot, lane = int(name[2]), "oq".index(name[1])
                off = slot * SLOT + lane * 128 + (1 - core) * 64
                there = ib.at[:, pl.ds(pl.multiple_of(off, 32), 64), :]
                pltpu.make_async_remote_copy(
                    src_ref=there,
                    dst_ref=there,
                    send_sem=send_sem.at[number],
                    recv_sem=recv_sem.at[number],
                    device_id=to,
                    device_id_type=pl.DeviceIdType.MESH,
                ).wait_recv()
            else:
                copy(name).wait_recv()

    own_rows = pl.ds(pl.multiple_of(core * 64, 64), 64)
    loads = [
        (txt_l.at[0], tb.at[0, pl.ds(0, 2 * HALF), :]),
        (txt_r.at[0], tb.at[1, pl.ds(0, 2 * HALF), :]),
        (img_l, ib.at[0, own_rows, :]),
        (img_r, ib.at[1, own_rows, :]),
        (isc_l, isc.at[0, 0]),
        (isc_r, isc.at[0, 1]),
        (pair, ipr.at[0]),
        (tsc_l, tsc.at[0, 0]),
        (tsc_r, tsc.at[0, 1]),
    ]
    loads = [pltpu.make_async_copy(s, d, local_sem.at[i]) for i, (s, d) in enumerate(loads)]
    for load in loads:
        load.start()
    barrier = pltpu.get_barrier_semaphore()
    near = (up_x, dn_x, up_y, dn_y)
    for to in near + (up_z, dn_z, other_core, diag):
        pl.semaphore_signal(barrier, inc=1, device_id=to, device_id_type=pl.DeviceIdType.MESH)
    for load in loads:
        load.wait()
    pl.semaphore_wait(barrier, 8)
    start("t1p", "t2p", "ip", "tsc", "isc", "ipr")
    start("io1+", "io1-", "t1o-", "t1o+", "t2o-", "t2o+", "so0")

    def tell(r):
        for to in near:
            pl.semaphore_signal(ready.at[r], inc=1, device_id=to, device_id_type=pl.DeviceIdType.MESH)

    def told(r):
        pl.semaphore_wait(ready.at[r], 4)

    tell(0)

    def source(piece):
        if piece in (0, 1, 2, 3):
            dx, dy, lane, half = 0, 0, piece // 2, piece % 2
        elif piece < 12:
            lane, half = (piece - 4) // 4, ((piece - 4) // 2) % 2
            step = 1 - 2 * (piece % 2)
            dx, dy = (0, step) if half == 0 else (step, 0)
        else:
            lane, half = piece % 2, (piece - 12) // 2
            dx, dy = (0, 2) if half == 0 else (2, 0)
        px = x_pair if (lane == 1 and half == 0) else wrap(x + dx, 4)
        py = y_pair if (lane == 1 and half == 1) else wrap(y + dy, 4)
        same = (half == 0 and lane == 0) or (half == 1 and dx % 2 == 0)
        return px, py, half, same

    def spread(which):
        @pl.loop(0, 24)
        def _(i):
            k, q = lax.div(i, 12), lax.rem(i, 12)
            line = tsc[which, k, pl.ds(q, 1), :]
            bc[which, k, pl.ds(pl.multiple_of(q * 128, 128), 128), :] = jnp.transpose(
                jnp.broadcast_to(line, (128, 128))
            )

    def text_setup(which):
        for piece in range(16):
            px, py, half, same = source(piece)
            if same != (which == 0):
                continue
            off = (lax.div(px, 2) * 4 + py) * 192 + half * HALF
            block = (z * 2 + lax.rem(px, 2)) * 2 + core
            base[piece] = block * 1536 + off
            for k in range(2):
                tcol[k, pl.ds(piece * HALF, HALF), :] = bc[which, k, pl.ds(pl.multiple_of(off, 32), HALF), :]

    def image_setup(lane):
        odd = x_odd if lane == 0 else 1 - x_odd
        lanes = pl.ds(lane * 128, 128)
        for slot, dz in enumerate(SLOT_Z):
            at = pl.ds(wrap(z + dz, 8) * 2 + odd, 1)
            irow[slot, 0:1, lanes] = isc[lane, 0, at, :] * (4.0 * LOG2E)
            irow[slot, 1:2, lanes] = isc[lane, 1, at, :] * (6.0 * LOG2E)
            iprow[slot, 0:1, lanes] = ipr[lane, at, :]

    def tile(k):
        early, late = lax.div(k - 10, 5), lax.div(k - 20, 4)
        slot = jnp.where(k < 10, lax.div(k, 2), jnp.where(k < 20, k - 10 - 5 * early, 5 + late))
        chunk = jnp.where(k < 10, lax.rem(k, 2), jnp.where(k < 20, 2 + early, k - 20 - 4 * late))
        return slot, chunk

    def dots(k, dl, dr):
        slot, chunk = tile(k)
        rows = pl.ds(pl.multiple_of(chunk * CHUNK, CHUNK), CHUNK)
        cols = pl.ds(pl.multiple_of(slot * SLOT, SLOT), SLOT)
        for which, out in ((0, dl), (1, dr)):
            out[...] = lax.dot_general(
                tb[which, rows, :], ib[which, cols, :], (((1,), (1,)), ((), ())), preferred_element_type=F32
            )

    def scores(k, dl, dr):
        slot, chunk = tile(k)
        scale = irow[slot]
        a_learn = jnp.broadcast_to(scale[0:1], (8, SLOT))
        a_refer = jnp.broadcast_to(scale[1:2], (8, SLOT))
        wanted = jnp.broadcast_to(iprow[slot][0:1], (8, SLOT)) - lax.broadcasted_iota(jnp.int32, (8, SLOT), 0)
        total = rs[slot]
        for piece in range(4):
            here = wanted - base[chunk * 4 + piece]
            for g in range(HALF // 8):
                at = piece * HALF + g * 8
                rows = pl.ds(pl.multiple_of(chunk * CHUNK + at, 8), 8)
                b_learn, b_refer = tcol[0, rows, :], tcol[1, rows, :]
                d = score(
                    dl[at : at + 8, :],
                    dr[at : at + 8, :],
                    a_learn,
                    a_refer,
                    jnp.concatenate([b_learn, b_learn], axis=1),
                    jnp.concatenate([b_refer, b_refer], axis=1),
                    here == g * 8,
                    c_learn,
                    c_refer,
                )
                total = total + d
                cs[rows, :] = cs[rows, :] + (d[:, :128] + d[:, 128:])
        rs[slot] = total

    rs[...] = jnp.zeros_like(rs)
    cs[...] = jnp.zeros_like(cs)
    spread(0)
    text_setup(0)
    image_setup(0)

    def near_z():
        got("io1+", "io1-")
        start("io2+", "io2-", "so1", "so2")

    def diag_in():
        got("ip")
        start("iq1+", "iq1-", "sq0")

    def near_text():
        for name in ("t1", "t2"):
            got(name + "o-", name + "o+")
            start(name + "o2-", name + "o2+")

    def pair_text():
        got("t1p")
        start("t1q-", "t1q+")
        got("t2p")
        start("t2q-", "t2q+")

    def second_z():
        got("io2+", "io2-")
        start("io3+", "io3-", "so3", "so4")

    def near_q():
        got("iq1+", "iq1-")
        start("iq2+", "iq2-", "sq1", "sq2")

    def near_pair_text():
        for name in ("t1", "t2"):
            got(name + "q-", name + "q+")
            start(name + "q2-", name + "q2+")

    def third_z():
        got("io3+", "io3-")
        start("io4+", "io4-", "so5", "so6")

    def second_q():
        got("iq2+", "iq2-")
        start("iq3+", "iq3-", "sq3", "sq4")

    def far_text():
        for name in ("t1", "t2"):
            got(name + "o2-", name + "o2+", name + "q2-", name + "q2+")

    def third_q():
        got("iq3+", "iq3-")
        start("iq4+", "iq4-", "sq5", "sq6")

    def far_z():
        got("io4+", "io4-")
        start("so7")

    def far_q():
        got("iq4+", "iq4-")
        start("sq7")

    near_z()
    diag_in()
    got("tsc", "isc", "ipr")
    spread(1)
    text_setup(1)
    image_setup(1)
    near_text()
    pair_text()
    got("so0", "sq0")
    told(0)
    tell(1)

    def events(k):
        if k == 2:
            second_z()
            near_q()
            got("so1", "sq1")
        elif k == 4:
            got("so2", "sq2")
        elif k == 6:
            third_z()
            second_q()
            got("so3", "sq3")
            told(1)
            tell(2)
        elif k == 8:
            got("so4", "sq4")
        elif k == 10:
            near_pair_text()
        elif k == 12:
            third_q()
        elif k == 15:
            far_text()
        elif k == 16:
            far_z()
        elif k == 20:
            got("so5", "sq5")
        elif k == 24:
            got("so6", "sq6")
            told(2)
        elif k == 28:
            far_q()
            got("so7", "sq7")

    times = (2, 4, 6, 8, 10, 12, 15, 16, 20, 24, 28)

    def at_step(k, odd):
        for t in times:
            if t % 2 == odd:

                @pl.when(k == t)
                def _(t=t):
                    events(t)

    dots(0, dl0, dr0)

    @pl.loop(0, STEPS // 2 - 1)
    def _(i):
        at_step(2 * i + 1, 1)
        dots(2 * i + 1, dl1, dr1)
        scores(2 * i, dl0, dr0)
        at_step(2 * i + 2, 0)
        dots(2 * i + 2, dl0, dr0)
        scores(2 * i + 1, dl1, dr1)

    dots(STEPS - 1, dl1, dr1)
    scores(STEPS - 2, dl0, dr0)
    scores(STEPS - 1, dl1, dr1)

    def row_copy(slot, lane, which):
        number = (slot * 2 + lane) * 2 + which
        if lane == 0:
            to = device(dz=SLOT_Z[slot], at_core=core if which == 0 else 1 - core)
        else:
            to = device(dz=SLOT_Z[slot], at_x=x_diag, at_y=y_diag, at_core=core if which == 0 else 1 - core)
        return pltpu.make_async_remote_copy(
            src_ref=row_part.at[slot * 2 + lane],
            dst_ref=row_recv.at[number],
            send_sem=row_send.at[number],
            recv_sem=row_got.at[number],
            device_id=to,
            device_id_type=pl.DeviceIdType.MESH,
        )

    for slot in (7, 6, 5, 4, 3, 2, 1, 0):
        line = jnp.sum(rs[slot], axis=0, keepdims=True) * LN2
        row_part[slot * 2] = line[:, :128]
        row_part[slot * 2 + 1] = line[:, 128:]
        for lane in (1, 0):
            for which in (1, 0):
                if (slot, lane, which) != (0, 0, 0):
                    row_copy(slot, lane, which).start()

    mine = x * 4 + y
    for piece in range(16):
        px, py, half, same = source(piece)
        line = jnp.sum(jnp.transpose(cs[pl.ds(piece * HALF, HALF), :]), axis=0, keepdims=True) * LN2
        place = py if half == 0 else 4 + lax.div(px, 2) * 2 + lax.rem(py, 2)
        col_part[0 if same else 1, place, :, 0:HALF] = line

    def col_copy(dx, dy):
        number = dx * 4 + dy - 1
        return pltpu.make_async_remote_copy(
            src_ref=col_part.at[dx % 2],
            dst_ref=col_recv.at[mine],
            send_sem=col_send.at[number],
            recv_sem=col_got.at[number],
            device_id=device(dx=dx, dy=dy),
            device_id_type=pl.DeviceIdType.MESH,
        )

    plane = [(dx, dy) for dx in range(4) for dy in range(4) if (dx, dy) != (0, 0)]
    for dx, dy in sorted(plane, key=lambda d: -(min(d[0], 4 - d[0]) + min(d[1], 4 - d[1]))):
        col_copy(dx, dy).start()
    col_recv[mine] = col_part[0]
    row_recv[0] = row_part[0]

    for slot in range(8):
        for lane in range(2):
            for which in range(2):
                if (slot, lane, which) != (0, 0, 0):
                    row_copy(slot, lane, which).wait_recv()
    line = row_recv[0]
    for number in range(1, 32):
        line = line + row_recv[number]
    row_out[...] = jnp.where(core == 0, line[:, :64], line[:, 64:])
    for dx, dy in plane:
        col_copy(dx, dy).wait_recv()
    for x_hi in range(2):
        for yy in range(4):
            at = [(2 * x_hi + a) * 4 + b for a in range(2) for b in range(4)]
            col_out[pl.ds((x_hi * 4 + yy) * 2, 1), :] = functools.reduce(
                lambda s, t: s + t, [col_recv[n, yy] for n in at]
            )
        for y_hi in range(2):
            for y_low in range(2):
                at = [a * 4 + 2 * y_hi + b for a in range(4) for b in range(2)]
                col_out[pl.ds((x_hi * 4 + y_hi * 2 + y_low) * 2 + 1, 1), :] = functools.reduce(
                    lambda s, t: s + t, [col_recv[n, 4 + x_hi * 2 + y_low] for n in at]
                )

    for name in messages:
        copy(name).wait_send()
    for slot in range(8):
        for lane in range(2):
            for which in range(2):
                if (slot, lane, which) != (0, 0, 0):
                    row_copy(slot, lane, which).wait_send()
    for dx, dy in plane:
        col_copy(dx, dy).wait_send()


def shards(
    image_learn,
    image_refer,
    text_learn,
    text_refer,
    image_scale_learn,
    image_scale_refer,
    text_scale_learn,
    text_scale_refer,
    pair_index,
):
    offset = math.log(text_scale_learn.shape[0] * lax.axis_size("col"))
    vmem, dma = pltpu.VMEM, pltpu.SemaphoreType.DMA
    any_space = pl.BlockSpec(memory_space=pl.ANY)
    rows, cols = pl.pallas_call(
        functools.partial(kernel, (1.0 - offset) * LOG2E, (-1.0 - offset) * LOG2E),
        out_shape=[jax.ShapeDtypeStruct((1, 64), F32), jax.ShapeDtypeStruct((16, 128), F32)],
        in_specs=[any_space] * 9,
        out_specs=[pl.BlockSpec(memory_space=vmem)] * 2,
        scratch_shapes=[
            vmem((2, 4 * CHUNK, E), jnp.bfloat16),
            vmem((2, 8 * SLOT, E), jnp.bfloat16),
            vmem((2, 2, 16, 128), F32),
            vmem((2, 16, 128), jnp.int32),
            vmem((2, 2, 12, 128), F32),
            vmem((2, 2, 1536, 128), F32),
            vmem((2, 4 * CHUNK, 128), F32),
            vmem((8, 8, SLOT), F32),
            vmem((8, 8, SLOT), jnp.int32),
            pltpu.SMEM((16,), jnp.int32),
            vmem((8, 8, SLOT), F32),
            vmem((4 * CHUNK, 128), F32),
            vmem((CHUNK, SLOT), F32),
            vmem((CHUNK, SLOT), F32),
            vmem((CHUNK, SLOT), F32),
            vmem((CHUNK, SLOT), F32),
            vmem((16, 1, 128), F32),
            vmem((32, 1, 128), F32),
            vmem((2, 8, 1, 128), F32),
            vmem((16, 8, 1, 128), F32),
            dma((9,)),
            dma((54,)),
            dma((54,)),
            dma((32,)),
            dma((32,)),
            dma((15,)),
            dma((15,)),
            pltpu.SemaphoreType.REGULAR((3,)),
        ],
        compiler_params=pltpu.CompilerParams(
            collective_id=0, has_side_effects=True, vmem_limit_bytes=44 * 2**20
        ),
        cost_estimate=pl.CostEstimate(
            flops=4 * 2048 * 1536 * E, bytes_accessed=2**21, transcendentals=3 * 2048 * 1536
        ),
        name="gather_score",
    )(
        image_learn,
        image_refer,
        text_learn,
        text_refer,
        image_scale_learn.reshape(16, 128),
        image_scale_refer.reshape(16, 128),
        text_scale_learn.reshape(12, 128),
        text_scale_refer.reshape(12, 128),
        pair_index.reshape(16, 128),
    )
    return rows.reshape(64), cols[:, :HALF].reshape(1536)


def solution(mesh):
    in_specs = (
        P(("grp", "col"), None),
        P(("grp", "col"), None),
        P("col", "grp", None),
        P("col", "grp", None),
        P("grp"),
        P("grp"),
        P("col"),
        P("col"),
        P("grp"),
    )
    out_specs = (P(("grp", "col")), P("col"))
    return jax.shard_map(shards, mesh=mesh, in_specs=in_specs, out_specs=out_specs, check_vma=False)
```

```python
import functools
import math

import jax
import jax.numpy as jnp
from jax import lax
from jax.experimental import pallas as pl
from jax.experimental.pallas import tpu as pltpu
from jax.sharding import PartitionSpec as P

F32 = jnp.float32
LOG2E = 1.0 / math.log(2.0)
LN2 = math.log(2.0)
SERIES = tuple(2.0 * LOG2E * c for c in (0.99999984, 0.33337989, 0.1979503, 0.17111227))

E = 1152
HALF = 96
CHUNK = 4 * HALF
BLOCK = 256
PIECE_Z = (0, 0, 1, -1, 1, -1, 2, -2, 2, -2, 3, -3, 3, -3, 4, 4)
PIECE_LANE = (0, 1, 0, 0, 1, 1, 0, 0, 1, 1, 0, 0, 1, 1, 0, 1)
STEPS = 32


def wrap(value, size):
    return lax.rem(value + size, size)


def score(dot_learn, dot_refer, a_learn, a_refer, b_learn, b_refer, paired, c_learn, c_refer):
    u = dot_learn * a_learn * b_learn + c_learn
    w = dot_refer * a_refer * b_refer + c_refer
    p = jnp.exp2(-jnp.abs(u))
    q = jnp.exp2(-jnp.abs(w))
    z = (p - q) * pl.reciprocal((p + q) + 2.0, approx=True)
    s = z * z
    poly = s * SERIES[3] + SERIES[2]
    poly = poly * s + SERIES[1]
    poly = poly * s + SERIES[0]
    d = (jnp.maximum(u, 0.0) - jnp.maximum(w, 0.0)) + z * poly
    return d - jnp.where(paired, u - w, 0.0)


def kernel(
    c_learn,
    c_refer,
    img_l,
    img_r,
    txt_l,
    txt_r,
    isc_l,
    isc_r,
    tsc_l,
    tsc_r,
    pair,
    row_out,
    col_out,
    tb,
    ib,
    isc,
    ipr,
    tsc,
    bc,
    tcol,
    irow,
    iprow,
    base,
    rs,
    cs,
    dl0,
    dr0,
    dl1,
    dr1,
    row_part,
    row_recv,
    col_part,
    col_recv,
    local_sem,
    send_sem,
    recv_sem,
    row_sem,
    col_sem,
    ready,
):
    grp, col = lax.axis_index("grp"), lax.axis_index("col")
    x = lax.div(grp, 4) * 2 + lax.rem(lax.div(col, 2), 2)
    y = lax.rem(grp, 4)
    z = lax.div(col, 4)
    core = lax.rem(col, 2)
    x_odd, y_odd = lax.rem(x, 2), lax.rem(y, 2)
    x_pair, y_pair = x + 1 - 2 * x_odd, y + 1 - 2 * y_odd
    x_diag, y_diag = wrap(x - 1 + 2 * x_odd, 4), wrap(y - 1 + 2 * y_odd, 4)

    def device(dx=0, dy=0, dz=0, at_x=None, at_y=None, at_core=None):
        px = wrap(x + dx, 4) if at_x is None else at_x
        py = wrap(y + dy, 4) if at_y is None else at_y
        pz = wrap(z + dz, 8)
        pc = core if at_core is None else at_core
        return lax.div(px, 2) * 4 + py, (pz * 2 + lax.rem(px, 2)) * 2 + pc

    other_core = device(at_core=1 - core)
    diag = device(at_x=x_diag, at_y=y_diag)
    pair_x, next_x = device(at_x=x_pair), device(at_x=x_diag)
    pair_y, next_y = device(at_y=y_pair), device(at_y=y_diag)
    up_z, dn_z = device(dz=1), device(dz=-1)

    messages = {}

    def message(name, src, dst, to):
        messages[name] = (len(messages), src, dst, to)

    def text(piece, part=None):
        off, rows = (piece * HALF, HALF) if part is None else (piece * HALF + part * (HALF // 2), HALF // 2)
        return tb.at[:, pl.ds(off, rows), :]

    def image(piece, part=None):
        rows = 64 if part is None else 32
        off = piece * 128 + core * 64 + (0 if part is None else part * 32)
        return ib.at[:, pl.ds(pl.multiple_of(off, 32), rows), :]

    message("tsc", tsc.at[0], tsc.at[1], pair_x)
    message("isc", isc.at[0], isc.at[1], diag)
    message("ipr", ipr.at[0], ipr.at[1], diag)
    message("t1p", text(0), text(2), pair_x)
    message("t2p", text(1), text(3), pair_y)
    message("ip", image(0), image(1), diag)
    for name, first, to_p, to_n in (("t1", 0, pair_y, next_y), ("t2", 1, pair_x, next_x)):
        o, far = 4 + 2 * first, 12 + first
        message(name + "oP", text(first), text(o), to_p)
        message(name + "oN", text(first), text(o + 1), to_n)
        message(name + "qP", text(2 + first), text(o + 4), to_p)
        message(name + "qN", text(2 + first), text(o + 5), to_n)
        message(name + "o2A", text(o, 0), text(far, 0), to_n)
        message(name + "o2B", text(o + 1, 1), text(far, 1), to_p)
        message(name + "q2A", text(o + 4, 0), text(far + 2, 0), to_n)
        message(name + "q2B", text(o + 5, 1), text(far + 2, 1), to_p)
    for lane, mark in ((0, "o"), (1, "q")):
        place = {dz: p for p, dz in enumerate(PIECE_Z) if PIECE_LANE[p] == lane}
        for k in (1, 2, 3):
            message(f"i{mark}{k}+", image(place[k - 1]), image(place[k]), dn_z)
            message(f"i{mark}{k}-", image(place[1 - k]), image(place[-k]), up_z)
        message(f"i{mark}4+", image(place[3], 0), image(place[4], 0), dn_z)
        message(f"i{mark}4-", image(place[-3], 1), image(place[4], 1), up_z)
    for piece in range(16):
        message(f"s{piece}", image(piece), image(piece), other_core)

    def sender(name):
        return {"tsc": 2, "isc": 3, "ipr": 4}.get(name, 0 if name[0] == "t" else 1)

    def copy(name):
        number, src, dst, to = messages[name]
        return pltpu.make_async_remote_copy(
            src_ref=src,
            dst_ref=dst,
            send_sem=send_sem.at[sender(name)],
            recv_sem=recv_sem.at[number],
            device_id=to,
            device_id_type=pl.DeviceIdType.MESH,
        )

    def start(*names):
        for name in names:
            copy(name).start()

    def got(*names):
        for name in names:
            if name[0] == "s":
                number, _, _, to = messages[name]
                off = int(name[1:]) * 128 + (1 - core) * 64
                there = ib.at[:, pl.ds(pl.multiple_of(off, 32), 64), :]
                pltpu.make_async_remote_copy(
                    src_ref=there,
                    dst_ref=there,
                    send_sem=send_sem.at[sender(name)],
                    recv_sem=recv_sem.at[number],
                    device_id=to,
                    device_id_type=pl.DeviceIdType.MESH,
                ).wait_recv()
            else:
                copy(name).wait_recv()

    own_rows = pl.ds(pl.multiple_of(core * 64, 64), 64)
    loads = [
        (0, txt_l.at[0], tb.at[0, pl.ds(0, 2 * HALF), :]),
        (0, txt_r.at[0], tb.at[1, pl.ds(0, 2 * HALF), :]),
        (1, img_l, ib.at[0, own_rows, :]),
        (1, img_r, ib.at[1, own_rows, :]),
        (2, isc_l, isc.at[0, 0]),
        (2, isc_r, isc.at[0, 1]),
        (3, tsc_l, tsc.at[0, 0]),
        (3, tsc_r, tsc.at[0, 1]),
        (4, pair, ipr.at[0]),
    ]
    for number, src, dst in loads:
        pltpu.make_async_copy(src, dst, local_sem.at[number]).start()

    def all_of(ref, sem):
        pltpu.make_async_copy(ref, ref, sem).wait()

    barrier = pltpu.get_barrier_semaphore()
    near = (pair_x, next_x, pair_y, next_y)
    for to in near + (up_z, dn_z, other_core, diag):
        pl.semaphore_signal(barrier, inc=1, device_id=to, device_id_type=pl.DeviceIdType.MESH)
    for number, ref in enumerate((tb.at[:, pl.ds(0, 2 * HALF), :], ib.at[:, own_rows, :], isc.at[0], tsc.at[0], ipr.at[0])):
        all_of(ref, local_sem.at[number])
    pl.semaphore_wait(barrier, 8)
    start("tsc", "isc", "ipr", "t1p", "t2p", "ip", "io1+", "io1-", "t1oP", "t2oP", "s0")

    def tell(r):
        for to in near:
            pl.semaphore_signal(ready.at[r], inc=1, device_id=to, device_id_type=pl.DeviceIdType.MESH)

    def told(r):
        pl.semaphore_wait(ready.at[r], 4)

    tell(0)

    def source(piece):
        if piece < 4:
            lane, half, side = piece // 2, piece % 2, 0
        elif piece < 12:
            lane, half, side = (piece - 4) // 4, ((piece - 4) // 2) % 2, 1 + piece % 2
        else:
            lane, half, side = (piece - 12) // 2, piece % 2, 3
        along_x, along_y = (x, x_pair, x_diag, wrap(x + 2, 4)), (y, y_pair, y_diag, wrap(y + 2, 4))
        px = along_x[side] if half == 1 else along_x[lane]
        py = along_y[side] if half == 0 else along_y[lane]
        same = lane == 0 if half == 0 else side in (0, 3)
        return px, py, half, same

    def spread(which):
        @pl.loop(0, 24)
        def _(i):
            k, q = lax.div(i, 12), lax.rem(i, 12)
            line = tsc[which, k, pl.ds(q, 1), :]
            bc[which, k, pl.ds(pl.multiple_of(q * 128, 128), 128), :] = jnp.transpose(
                jnp.broadcast_to(line, (128, 128))
            )

    def text_setup(which):
        for piece in range(16):
            px, py, half, same = source(piece)
            if same != (which == 0):
                continue
            off = (lax.div(px, 2) * 4 + py) * 192 + half * HALF
            block = (z * 2 + lax.rem(px, 2)) * 2 + core
            base[piece] = block * 1536 + off
            for k in range(2):
                tcol[k, pl.ds(piece * HALF, HALF), :] = bc[which, k, pl.ds(pl.multiple_of(off, 32), HALF), :]

    def image_setup(lane):
        odd = x_odd if lane == 0 else 1 - x_odd
        for piece in range(16):
            if PIECE_LANE[piece] != lane:
                continue
            block, lanes = piece // 2, pl.ds((piece % 2) * 128, 128)
            at = pl.ds(wrap(z + PIECE_Z[piece], 8) * 2 + odd, 1)
            irow[block, 0:1, lanes] = isc[lane, 0, at, :] * (4.0 * LOG2E)
            irow[block, 1:2, lanes] = isc[lane, 1, at, :] * (6.0 * LOG2E)
            iprow[block, 0:1, lanes] = ipr[lane, at, :]

    def tile(k):
        block = jnp.where(
            k < 18,
            jnp.where(
                k < 8,
                jnp.where(k < 6, lax.rem(k, 3), 3),
                jnp.where(k < 12, k - 8, lax.div(k, 3)),
            ),
            jnp.where(k < 26, jnp.where(k < 22, k - 18, 6), jnp.where(k < 28, k - 22, 7)),
        )
        chunk = jnp.where(
            k < 18,
            jnp.where(k < 8, jnp.where(k < 6, lax.div(k, 3), k - 6), jnp.where(k < 12, 2, lax.rem(k, 3))),
            jnp.where(k < 26, jnp.where(k < 22, 3, k - 22), jnp.where(k < 28, 3, k - 28)),
        )
        return block, chunk

    def dots(k, dl, dr):
        block, chunk = tile(k)
        rows = pl.ds(pl.multiple_of(chunk * CHUNK, CHUNK), CHUNK)
        cols = pl.ds(pl.multiple_of(block * BLOCK, BLOCK), BLOCK)
        for which, out in ((0, dl), (1, dr)):
            out[...] = lax.dot_general(
                tb[which, rows, :], ib[which, cols, :], (((1,), (1,)), ((), ())), preferred_element_type=F32
            )

    def scores(k, dl, dr):
        block, chunk = tile(k)
        scale = irow[block]
        a_learn = jnp.broadcast_to(scale[0:1], (8, BLOCK))
        a_refer = jnp.broadcast_to(scale[1:2], (8, BLOCK))
        wanted = jnp.broadcast_to(iprow[block][0:1], (8, BLOCK)) - lax.broadcasted_iota(jnp.int32, (8, BLOCK), 0)
        total = rs[block]
        for piece in range(4):
            here = wanted - base[chunk * 4 + piece]
            for g in range(HALF // 8):
                at = piece * HALF + g * 8
                rows = pl.ds(pl.multiple_of(chunk * CHUNK + at, 8), 8)
                b_learn, b_refer = tcol[0, rows, :], tcol[1, rows, :]
                d = score(
                    dl[at : at + 8, :],
                    dr[at : at + 8, :],
                    a_learn,
                    a_refer,
                    jnp.concatenate([b_learn, b_learn], axis=1),
                    jnp.concatenate([b_refer, b_refer], axis=1),
                    here == g * 8,
                    c_learn,
                    c_refer,
                )
                total = total + d
                cs[rows, :] = cs[rows, :] + (d[:, :128] + d[:, 128:])
        rs[block] = total

    rs[...] = jnp.zeros_like(rs)
    cs[...] = jnp.zeros_like(cs)
    spread(0)
    text_setup(0)
    image_setup(0)

    def row_copy(piece, which):
        number = piece * 2 + which
        at_core = core if which == 0 else 1 - core
        if PIECE_LANE[piece] == 0:
            to = device(dz=PIECE_Z[piece], at_core=at_core)
        else:
            to = device(dz=PIECE_Z[piece], at_x=x_diag, at_y=y_diag, at_core=at_core)
        return pltpu.make_async_remote_copy(
            src_ref=row_part.at[piece],
            dst_ref=row_recv.at[number],
            send_sem=row_sem.at[0],
            recv_sem=row_sem.at[1],
            device_id=to,
            device_id_type=pl.DeviceIdType.MESH,
        )

    row_messages = [(piece, which) for piece in range(16) for which in range(2) if (piece, which) != (0, 0)]

    def send_rows(blocks):
        for block in blocks:
            line = jnp.sum(rs[block], axis=0, keepdims=True) * LN2
            row_part[block * 2] = line[:, :128]
            row_part[block * 2 + 1] = line[:, 128:]
        for piece, which in reversed(row_messages):
            if piece // 2 in blocks:
                row_copy(piece, which).start()

    got("tsc", "isc", "ipr")
    spread(1)
    text_setup(1)
    image_setup(1)
    got("io1+", "io1-")
    start("s2", "s3")
    got("ip")
    start("iq1+", "iq1-", "io2+", "io2-", "s1", "t1oN", "t2oN")
    told(0)
    tell(1)
    got("t1p", "t2p")
    start("t1qP", "t2qP", "t1qN", "t2qN")
    got("s0", "s1", "s2", "s3")

    def events(i):
        if i == 1:
            got("iq1+", "iq1-")
            start("iq2+", "iq2-", "s4", "s5")
            got("t1oN", "t2oN")
            start("t1o2B", "t2o2B")
            got("t1oP", "t2oP")
            start("t1o2A", "t2o2A")
            got("s4", "s5")
        elif i == 2:
            got("io2+", "io2-")
            start("io3+", "io3-", "s6", "s7")
        elif i == 3:
            got("s6", "s7")
            told(1)
            tell(2)
        elif i == 4:
            got("t1qN", "t2qN")
            start("t1q2B", "t2q2B")
            got("iq2+", "iq2-")
            start("iq3+", "iq3-", "s8", "s9")
            got("t1qP", "t2qP")
            start("t1q2A", "t2q2A")
        elif i == 6:
            got("s8", "s9")
        elif i == 7:
            got("io3+", "io3-")
            start("io4+", "io4-", "s10", "s11")
            got("s10", "s11")
        elif i == 9:
            got("t1o2A", "t1o2B", "t2o2A", "t2o2B", "t1q2A", "t1q2B", "t2q2A", "t2q2B")
        elif i == 10:
            got("iq3+", "iq3-")
            start("iq4+", "iq4-", "s12", "s13")
        elif i == 11:
            got("s12", "s13")
        elif i == 12:
            got("io4+", "io4-")
            start("s14")
        elif i == 13:
            told(2)
        elif i == 14:
            send_rows((0, 1, 2, 3, 4, 6))
            got("iq4+", "iq4-")
            start("s15")
            got("s14", "s15")

    dots(0, dl0, dr0)
    dots(1, dl1, dr1)
    scores(0, dl0, dr0)

    @pl.loop(1, STEPS // 2)
    def _(i):
        for low, high in ((1, 4), (4, 10), (10, 15)):

            @pl.when((i >= low) & (i < high))
            def _(low=low, high=high):
                for at in range(low, high):
                    if at not in (5, 8):

                        @pl.when(i == at)
                        def _(at=at):
                            events(at)

        dots(2 * i, dl0, dr0)
        scores(2 * i - 1, dl1, dr1)
        dots(2 * i + 1, dl1, dr1)
        scores(2 * i, dl0, dr0)

    scores(STEPS - 1, dl1, dr1)

    send_rows((5, 7))

    mine = x * 4 + y
    for piece in range(16):
        px, py, half, same = source(piece)
        line = jnp.sum(jnp.transpose(cs[pl.ds(piece * HALF, HALF), :]), axis=0, keepdims=True) * LN2
        place = py if half == 0 else 4 + lax.div(px, 2) * 2 + lax.rem(py, 2)
        col_part[0 if same else 1, place, :, 0:HALF] = line

    def col_copy(dx, dy):
        return pltpu.make_async_remote_copy(
            src_ref=col_part.at[dx % 2],
            dst_ref=col_recv.at[mine],
            send_sem=col_sem.at[0],
            recv_sem=col_sem.at[1],
            device_id=device(dx=dx, dy=dy),
            device_id_type=pl.DeviceIdType.MESH,
        )

    plane = [(dx, dy) for dx in range(4) for dy in range(4) if (dx, dy) != (0, 0)]
    for dx, dy in sorted(plane, key=lambda d: -(min(d[0], 4 - d[0]) + min(d[1], 4 - d[1]))):
        col_copy(dx, dy).start()
    col_recv[mine] = col_part[0]
    row_recv[0] = row_part[0]

    all_of(row_recv.at[pl.ds(0, 31)], row_sem.at[1])
    line = row_recv[0]
    for number in range(1, 32):
        line = line + row_recv[number]
    row_out[...] = jnp.where(core == 0, line[:, :64], line[:, 64:])
    all_of(col_recv.at[pl.ds(0, 15)], col_sem.at[1])
    for x_hi in range(2):
        for yy in range(4):
            at = [(2 * x_hi + a) * 4 + b for a in range(2) for b in range(4)]
            col_out[pl.ds((x_hi * 4 + yy) * 2, 1), :] = functools.reduce(
                lambda s, t: s + t, [col_recv[n, yy] for n in at]
            )
        for y_hi in range(2):
            for y_low in range(2):
                at = [a * 4 + 2 * y_hi + b for a in range(4) for b in range(2)]
                col_out[pl.ds((x_hi * 4 + y_hi * 2 + y_low) * 2 + 1, 1), :] = functools.reduce(
                    lambda s, t: s + t, [col_recv[n, 4 + x_hi * 2 + y_low] for n in at]
                )

    all_of(tb.at[:, pl.ds(0, 14 * HALF), :], send_sem.at[0])
    all_of(ib.at[:, pl.ds(0, 31 * 64), :], send_sem.at[1])
    all_of(tsc.at[0], send_sem.at[2])
    all_of(isc.at[0], send_sem.at[3])
    all_of(ipr.at[0], send_sem.at[4])
    all_of(row_recv.at[pl.ds(0, 31)], row_sem.at[0])
    all_of(col_recv.at[pl.ds(0, 15)], col_sem.at[0])


def shards(
    image_learn,
    image_refer,
    text_learn,
    text_refer,
    image_scale_learn,
    image_scale_refer,
    text_scale_learn,
    text_scale_refer,
    pair_index,
):
    offset = math.log(text_scale_learn.shape[0] * lax.axis_size("col"))
    vmem, dma = pltpu.VMEM, pltpu.SemaphoreType.DMA
    in_hbm = pl.BlockSpec(memory_space=pltpu.HBM)
    rows, cols = pl.pallas_call(
        functools.partial(kernel, (1.0 - offset) * LOG2E, (-1.0 - offset) * LOG2E),
        out_shape=[jax.ShapeDtypeStruct((1, 64), F32), jax.ShapeDtypeStruct((16, 128), F32)],
        in_specs=[in_hbm] * 9,
        out_specs=[pl.BlockSpec(memory_space=vmem)] * 2,
        scratch_shapes=[
            vmem((2, 4 * CHUNK, E), jnp.bfloat16),
            vmem((2, 8 * BLOCK, E), jnp.bfloat16),
            vmem((2, 2, 16, 128), F32),
            vmem((2, 16, 128), jnp.int32),
            vmem((2, 2, 12, 128), F32),
            vmem((2, 2, 1536, 128), F32),
            vmem((2, 4 * CHUNK, 128), F32),
            vmem((8, 8, BLOCK), F32),
            vmem((8, 8, BLOCK), jnp.int32),
            pltpu.SMEM((16,), jnp.int32),
            vmem((8, 8, BLOCK), F32),
            vmem((4 * CHUNK, 128), F32),
            vmem((CHUNK, BLOCK), F32),
            vmem((CHUNK, BLOCK), F32),
            vmem((CHUNK, BLOCK), F32),
            vmem((CHUNK, BLOCK), F32),
            vmem((16, 1, 128), F32),
            vmem((32, 1, 128), F32),
            vmem((2, 8, 1, 128), F32),
            vmem((16, 8, 1, 128), F32),
            dma((5,)),
            dma((5,)),
            dma((54,)),
            dma((2,)),
            dma((2,)),
            pltpu.SemaphoreType.REGULAR((3,)),
        ],
        compiler_params=pltpu.CompilerParams(
            collective_id=0, has_side_effects=True, vmem_limit_bytes=60 * 2**20
        ),
        cost_estimate=pl.CostEstimate(
            flops=4 * 2048 * 1536 * E, bytes_accessed=2**21, transcendentals=3 * 2048 * 1536
        ),
        name="gather_score",
    )(
        image_learn,
        image_refer,
        text_learn,
        text_refer,
        image_scale_learn.reshape(16, 128),
        image_scale_refer.reshape(16, 128),
        text_scale_learn.reshape(12, 128),
        text_scale_refer.reshape(12, 128),
        pair_index.reshape(16, 128),
    )
    return rows.reshape(64), cols[:, :HALF].reshape(1536)


def solution(mesh):
    in_specs = (
        P(("grp", "col"), None),
        P(("grp", "col"), None),
        P("col", "grp", None),
        P("col", "grp", None),
        P("grp"),
        P("grp"),
        P("col"),
        P("col"),
        P("grp"),
    )
    out_specs = (P(("grp", "col")), P("col"))
    return jax.shard_map(shards, mesh=mesh, in_specs=in_specs, out_specs=out_specs, check_vma=False)
```

```python
import functools
import math

import jax
import jax.numpy as jnp
from jax import lax
from jax.experimental import pallas as pl
from jax.experimental.pallas import tpu as pltpu
from jax.sharding import PartitionSpec as P

F32 = jnp.float32
LOG2E = 1.0 / math.log(2.0)
LN2 = math.log(2.0)
SERIES = tuple(2.0 * LOG2E * c for c in (0.99999984, 0.33337989, 0.1979503, 0.17111227))

E = 1152
HALF = 96
CHUNK = 4 * HALF
SPLIT = {1: 1024, 2: 1024, 3: 1024, 4: 1024}
BLOCK = 256
PIECE_Z = (0, 0, 1, -1, 1, -1, 2, -2, 2, -2, 3, -3, 3, -3, 4, 4)
PIECE_LANE = (0, 1, 0, 0, 1, 1, 0, 0, 1, 1, 0, 0, 1, 1, 0, 1)
STEPS = 32


def wrap(value, size):
    return lax.rem(value + size, size)


def score(dot_learn, dot_refer, a_learn, a_refer, b_learn, b_refer, paired, c_learn, c_refer):
    u = dot_learn * a_learn * b_learn + c_learn
    w = dot_refer * a_refer * b_refer + c_refer
    p = jnp.exp2(-jnp.abs(u))
    q = jnp.exp2(-jnp.abs(w))
    z = (p - q) * pl.reciprocal((p + q) + 2.0, approx=True)
    s = z * z
    poly = s * SERIES[3] + SERIES[2]
    poly = poly * s + SERIES[1]
    poly = poly * s + SERIES[0]
    d = (jnp.maximum(u, 0.0) - jnp.maximum(w, 0.0)) + z * poly
    return d - jnp.where(paired, u - w, 0.0)


def kernel(
    c_learn,
    c_refer,
    img_l,
    img_r,
    txt_l,
    txt_r,
    isc_l,
    isc_r,
    tsc_l,
    tsc_r,
    pair,
    row_out,
    col_out,
    tb,
    ib,
    isc,
    ipr,
    tsc,
    bc,
    tcol,
    irow,
    iprow,
    base,
    rs,
    cs,
    dl0,
    dr0,
    dl1,
    dr1,
    row_part,
    row_recv,
    col_part,
    col_recv,
    local_sem,
    send_sem,
    recv_sem,
    row_sem,
    col_sem,
    ready,
):
    grp, col = lax.axis_index("grp"), lax.axis_index("col")
    x = lax.div(grp, 4) * 2 + lax.rem(lax.div(col, 2), 2)
    y = lax.rem(grp, 4)
    z = lax.div(col, 4)
    core = lax.rem(col, 2)
    x_odd, y_odd = lax.rem(x, 2), lax.rem(y, 2)
    x_pair, y_pair = x + 1 - 2 * x_odd, y + 1 - 2 * y_odd
    x_diag, y_diag = wrap(x - 1 + 2 * x_odd, 4), wrap(y - 1 + 2 * y_odd, 4)

    def device(dx=0, dy=0, dz=0, at_x=None, at_y=None, at_core=None):
        px = wrap(x + dx, 4) if at_x is None else at_x
        py = wrap(y + dy, 4) if at_y is None else at_y
        pz = wrap(z + dz, 8)
        pc = core if at_core is None else at_core
        return lax.div(px, 2) * 4 + py, (pz * 2 + lax.rem(px, 2)) * 2 + pc

    other_core = device(at_core=1 - core)
    diag = device(at_x=x_diag, at_y=y_diag)
    pair_x, next_x = device(at_x=x_pair), device(at_x=x_diag)
    pair_y, next_y = device(at_y=y_pair), device(at_y=y_diag)
    up_z, dn_z = device(dz=1), device(dz=-1)

    groups, messages = {}, {}

    def group(name, ref):
        groups[name] = (len(groups), ref)

    def message(name, group_name, copies, to):
        messages[name] = (group_name, copies, to)

    def text(piece, start=0, rows=HALF):
        return tb.at[:, pl.ds(piece * HALF + start, rows), :]

    def image(piece, part=None, first=0, size=E):
        rows = 64 if part is None else 32
        off = piece * 128 + core * 64 + (0 if part is None else part * 32)
        return ib.at[:, pl.ds(pl.multiple_of(off, 32), rows), pl.ds(first, size)]

    group("scales", bc.at[0, 0, pl.ds(0, 72), :])
    message("tsc", "scales", [(tsc_l, tsc.at[1, 0]), (tsc_r, tsc.at[1, 1])], pair_x)
    message("isc", "scales", [(isc_l, isc.at[1, 0]), (isc_r, isc.at[1, 1]), (pair, ipr.at[1])], diag)
    group("tp", tb.at[:, pl.ds(0, 192), :])
    first, second = pl.ds(0, HALF), pl.ds(HALF, HALF)
    message("t1p", "tp", [(t.at[0, first, :], text(2).at[i]) for i, t in enumerate((txt_l, txt_r))], pair_x)
    message("t2p", "tp", [(t.at[0, second, :], text(3).at[i]) for i, t in enumerate((txt_l, txt_r))], pair_y)
    group("ip", ib.at[:, pl.ds(0, 64), :])
    message("ip", "ip", [(r, image(1).at[i]) for i, r in enumerate((img_l, img_r))], diag)
    for name in ("oP", "oN", "qP", "qN"):
        group("t" + name, tb.at[:, pl.ds(0, 192), :])
    group("t2", tb.at[:, pl.ds(0, 384), :])
    for name, first, to_p, to_n in (("t1", 0, pair_y, next_y), ("t2", 1, pair_x, next_x)):
        o, far = 4 + 2 * first, 12 + first
        message(name + "oP", "toP", [(text(first), text(o))], to_p)
        for part, start_row, rows in (("a", 0, 32), ("b", 32, 64)):
            message(name + "oN" + part, "toN", [(text(first, start_row, rows), text(o + 1, start_row, rows))], to_n)
        message(name + "qP", "tqP", [(text(2 + first), text(o + 4))], to_p)
        message(name + "qN", "tqN", [(text(2 + first), text(o + 5))], to_n)
        message(name + "o2A", "t2", [(text(o, 0, 48), text(far, 0, 48))], to_n)
        message(name + "o2B", "t2", [(text(o + 1, 48, 48), text(far, 48, 48))], to_p)
        message(name + "q2A", "t2", [(text(o + 4, 0, 48), text(far + 2, 0, 48))], to_n)
        message(name + "q2B", "t2", [(text(o + 5, 48, 48), text(far + 2, 48, 48))], to_p)
    for lane, mark in ((0, "o"), (1, "q")):
        place = {dz: p for p, dz in enumerate(PIECE_Z) if PIECE_LANE[p] == lane}
        for k in (1, 2, 3, 4):
            size = E if lane == 0 else SPLIT[k]
            ring = f"i{mark}{k}"
            if ring != "io1":
                group(ring, ib.at[:, pl.ds(0, 128 if k < 4 else 64), pl.ds(0, size)])
            if ring in ("io1", "io2"):
                for i, (part, own) in enumerate((("l", img_l), ("r", img_r))):
                    if ring == "io1":
                        group(ring + part, ib.at[0, pl.ds(0, 128), :])
                    for sign, to, at in (("+", dn_z, 1), ("-", up_z, -1)):
                        src = own if ring == "io1" else image(place[at]).at[i]
                        group_name = ring + part if ring == "io1" else ring
                        message(ring + part + sign, group_name, [(src, image(place[k * at]).at[i])], to)
            elif k < 4:
                message(ring + "+", ring, [(image(place[k - 1], size=size), image(place[k], size=size))], dn_z)
                message(ring + "-", ring, [(image(place[1 - k], size=size), image(place[-k], size=size))], up_z)
            else:
                message(ring + "+", ring, [(image(place[3], 0, size=size), image(place[4], 0, size=size))], dn_z)
                message(ring + "-", ring, [(image(place[-3], 1, size=size), image(place[4], 1, size=size))], up_z)
            if lane == 0 and SPLIT[k] < E:
                rest = dict(first=SPLIT[k], size=E - SPLIT[k])
                group(f"x{k}", ib.at[:, pl.ds(0, 128 if k < 4 else 64), pl.ds(0, E - SPLIT[k])])
                for at in (k, -k) if k < 4 else (k,):
                    there = [p for p in range(16) if PIECE_Z[p] == at and PIECE_LANE[p] == 1][0]
                    message(f"x{k}{at}", f"x{k}", [(image(place[at], **rest), image(there, **rest))], diag)
    for block in range(8):
        if block != 1:
            group(f"s{block}", ib.at[:, pl.ds(0, 128 if block else 256), :])
    for piece in range(16):
        message(f"s{piece}", f"s{piece // 2 if piece > 3 else 0}", [(image(piece), image(piece))], other_core)

    def sender(name):
        return 2 if name in ("tsc", "isc") else 0 if name[0] == "t" else 1

    def start(*names):
        for name in names:
            group_name, copies, to = messages[name]
            for src, dst in copies:
                pltpu.make_async_remote_copy(
                    src_ref=src,
                    dst_ref=dst,
                    send_sem=send_sem.at[sender(name)],
                    recv_sem=recv_sem.at[groups[group_name][0]],
                    device_id=to,
                    device_id_type=pl.DeviceIdType.MESH,
                ).start()

    def all_of(ref, sem):
        pltpu.make_async_copy(ref, ref, sem).wait()

    def got(*names):
        for name in names:
            number, ref = groups[name]
            all_of(ref, recv_sem.at[number])

    own_rows = pl.ds(pl.multiple_of(core * 64, 64), 64)
    barrier = pltpu.get_barrier_semaphore()
    near = (pair_x, next_x, pair_y, next_y)
    for to in near + (up_z, dn_z, other_core, diag):
        pl.semaphore_signal(barrier, inc=1, device_id=to, device_id_type=pl.DeviceIdType.MESH)
    loads = [
        (0, txt_l.at[0], tb.at[0, pl.ds(0, 2 * HALF), :]),
        (0, txt_r.at[0], tb.at[1, pl.ds(0, 2 * HALF), :]),
        (1, img_l, ib.at[0, own_rows, :]),
        (1, img_r, ib.at[1, own_rows, :]),
        (2, isc_l, isc.at[0, 0]),
        (2, isc_r, isc.at[0, 1]),
        (3, tsc_l, tsc.at[0, 0]),
        (3, tsc_r, tsc.at[0, 1]),
        (4, pair, ipr.at[0]),
    ]
    for number, src, dst in loads:
        pltpu.make_async_copy(src, dst, local_sem.at[number]).start()

    pl.semaphore_wait(barrier, 8)
    start("tsc", "isc", "ip", "t1p", "t2p", "io1l+", "io1l-", "io1r+", "io1r-")
    for number, ref in enumerate((tb.at[:, pl.ds(0, 2 * HALF), :], ib.at[:, own_rows, :], isc.at[0], tsc.at[0], ipr.at[0])):
        all_of(ref, local_sem.at[number])
    start("s0", "t1oNa", "t2oNa", "t2oNb", "t1oP", "t2oP")

    def tell(r):
        for to in near:
            pl.semaphore_signal(ready.at[r], inc=1, device_id=to, device_id_type=pl.DeviceIdType.MESH)

    def told(r):
        pl.semaphore_wait(ready.at[r], 4)

    tell(0)

    def source(piece):
        if piece < 4:
            lane, half, side = piece // 2, piece % 2, 0
        elif piece < 12:
            lane, half, side = (piece - 4) // 4, ((piece - 4) // 2) % 2, 1 + piece % 2
        else:
            lane, half, side = (piece - 12) // 2, piece % 2, 3
        along_x, along_y = (x, x_pair, x_diag, wrap(x + 2, 4)), (y, y_pair, y_diag, wrap(y + 2, 4))
        px = along_x[side] if half == 1 else along_x[lane]
        py = along_y[side] if half == 0 else along_y[lane]
        same = lane == 0 if half == 0 else side in (0, 3)
        return px, py, half, same

    def spread(which):
        @pl.loop(0, 24)
        def _(i):
            k, q = lax.div(i, 12), lax.rem(i, 12)
            line = tsc[which, k, pl.ds(q, 1), :]
            bc[which, k, pl.ds(pl.multiple_of(q * 128, 128), 128), :] = jnp.transpose(
                jnp.broadcast_to(line, (128, 128))
            )

    def text_setup(which):
        for piece in range(16):
            px, py, half, same = source(piece)
            if same != (which == 0):
                continue
            off = (lax.div(px, 2) * 4 + py) * 192 + half * HALF
            block = (z * 2 + lax.rem(px, 2)) * 2 + core
            base[piece] = block * 1536 + off
            for k in range(2):
                tcol[k, pl.ds(piece * HALF, HALF), :] = bc[which, k, pl.ds(pl.multiple_of(off, 32), HALF), :]

    def image_setup(lane):
        odd = x_odd if lane == 0 else 1 - x_odd
        for piece in range(16):
            if PIECE_LANE[piece] != lane:
                continue
            block, lanes = piece // 2, pl.ds((piece % 2) * 128, 128)
            at = pl.ds(wrap(z + PIECE_Z[piece], 8) * 2 + odd, 1)
            irow[block, 0:1, lanes] = isc[lane, 0, at, :] * (4.0 * LOG2E)
            irow[block, 1:2, lanes] = isc[lane, 1, at, :] * (6.0 * LOG2E)
            iprow[block, 0:1, lanes] = ipr[lane, at, :]

    def tile(k):
        block = jnp.where(
            k < 18,
            jnp.where(
                k < 8,
                jnp.where(k < 6, lax.rem(k, 3), 3),
                jnp.where(k < 12, k - 8, lax.div(k, 3)),
            ),
            jnp.where(k < 24, jnp.where(k < 22, k - 16, k - 22), lax.div(k, 4)),
        )
        chunk = jnp.where(
            k < 18,
            jnp.where(k < 8, jnp.where(k < 6, lax.div(k, 3), k - 6), jnp.where(k < 12, 2, lax.rem(k, 3))),
            jnp.where(k < 24, 3, lax.rem(k, 4)),
        )
        return block, chunk

    def dots(k, dl, dr):
        block, chunk = tile(k)
        rows = pl.ds(pl.multiple_of(chunk * CHUNK, CHUNK), CHUNK)
        cols = pl.ds(pl.multiple_of(block * BLOCK, BLOCK), BLOCK)
        for which, out in ((0, dl), (1, dr)):
            out[...] = lax.dot_general(
                tb[which, rows, :], ib[which, cols, :], (((1,), (1,)), ((), ())), preferred_element_type=F32
            )

    def scores(k, dl, dr):
        block, chunk = tile(k)
        scale = irow[block]
        a_learn = jnp.broadcast_to(scale[0:1], (8, BLOCK))
        a_refer = jnp.broadcast_to(scale[1:2], (8, BLOCK))
        wanted = jnp.broadcast_to(iprow[block][0:1], (8, BLOCK)) - lax.broadcasted_iota(jnp.int32, (8, BLOCK), 0)
        total = rs[block]
        for piece in range(4):
            here = wanted - base[chunk * 4 + piece]
            for g in range(HALF // 8):
                at = piece * HALF + g * 8
                rows = pl.ds(pl.multiple_of(chunk * CHUNK + at, 8), 8)
                b_learn, b_refer = tcol[0, rows, :], tcol[1, rows, :]
                d = score(
                    dl[at : at + 8, :],
                    dr[at : at + 8, :],
                    a_learn,
                    a_refer,
                    jnp.concatenate([b_learn, b_learn], axis=1),
                    jnp.concatenate([b_refer, b_refer], axis=1),
                    here == g * 8,
                    c_learn,
                    c_refer,
                )
                total = total + d
                cs[rows, :] = cs[rows, :] + (d[:, :128] + d[:, 128:])
        rs[block] = total

    rs[...] = jnp.zeros_like(rs)
    cs[...] = jnp.zeros_like(cs)
    spread(0)
    text_setup(0)
    image_setup(0)

    def row_copy(piece, which):
        number = piece * 2 + which
        at_core = core if which == 0 else 1 - core
        if PIECE_LANE[piece] == 0:
            to = device(dz=PIECE_Z[piece], at_core=at_core)
        else:
            to = device(dz=PIECE_Z[piece], at_x=x_diag, at_y=y_diag, at_core=at_core)
        return pltpu.make_async_remote_copy(
            src_ref=row_part.at[piece],
            dst_ref=row_recv.at[number],
            send_sem=row_sem.at[0],
            recv_sem=row_sem.at[1],
            device_id=to,
            device_id_type=pl.DeviceIdType.MESH,
        )

    row_messages = [(piece, which) for piece in range(16) for which in range(2) if (piece, which) != (0, 0)]

    def send_rows(blocks):
        for block in blocks:
            line = jnp.sum(rs[block], axis=0, keepdims=True) * LN2
            row_part[block * 2] = line[:, :128]
            row_part[block * 2 + 1] = line[:, 128:]
        for piece, which in reversed(row_messages):
            if piece // 2 in blocks:
                row_copy(piece, which).start()

    def sum_columns(pieces):
        for piece in pieces:
            px, py, half, same = source(piece)
            line = jnp.sum(jnp.transpose(cs[pl.ds(piece * HALF, HALF), :]), axis=0, keepdims=True) * LN2
            place = py if half == 0 else 4 + lax.div(px, 2) * 2 + lax.rem(py, 2)
            col_part[0 if same else 1, place, :, 0:HALF] = line

    got("scales")
    spread(1)
    got("io1l")
    start("io2l+", "io2l-")
    text_setup(1)
    image_setup(1)
    got("io1r")
    start("x11", "x1-1", "s2", "s3")
    got("ip")
    start("iq1+", "iq1-", "io2r+", "io2r-", "s1", "t1oNb")
    told(0)
    tell(1)
    got("tp")
    start("t1qP", "t2qP", "t1qN", "t2qN")
    got("s0")

    def events(i):
        if i == 1:
            got("iq1")
            start("iq2+", "iq2-")
            got("x1")
            start("s4", "s5")
            got("toN")
            start("t1o2B", "t2o2B")
            got("io2")
            start("x22", "x2-2", "s6", "s7", "io3+", "io3-")
            got("toP")
            start("t1o2A", "t2o2A")
            got("s2")
        elif i == 3:
            got("s3")
            told(1)
            tell(2)
        elif i == 4:
            got("iq2")
            start("iq3+", "iq3-")
            got("tqN")
            start("t1q2B", "t2q2B")
            got("tqP")
            start("t1q2A", "t2q2A")
        elif i == 5:
            got("x2")
            start("s8", "s9")
            got("io3")
            start("io4+", "io4-", "s10", "s11", "x33", "x3-3")
        elif i == 6:
            got("s4")
        elif i == 7:
            got("s5")
        elif i == 9:
            got("iq3")
            start("iq4+", "iq4-")
            got("t2")
        elif i == 10:
            got("io4")
            start("x44", "s14")
        elif i == 11:
            got("x3")
            start("s12", "s13")
        elif i == 12:
            told(2)
            send_rows((0, 2, 3, 4, 5))
            got("s6")
        elif i == 13:
            got("iq4", "x4")
            start("s15")
        elif i == 14:
            send_rows((1,))
            got("s7")

    dots(0, dl0, dr0)
    dots(1, dl1, dr1)
    scores(0, dl0, dr0)

    @pl.loop(1, STEPS // 2 - 1)
    def _(i):
        for low, high in ((1, 4), (4, 10), (10, 15)):

            @pl.when((i >= low) & (i < high))
            def _(low=low, high=high):
                for at in range(low, high):
                    if at not in (2, 8):

                        @pl.when(i == at)
                        def _(at=at):
                            events(at)

        dots(2 * i, dl0, dr0)
        scores(2 * i - 1, dl1, dr1)
        dots(2 * i + 1, dl1, dr1)
        scores(2 * i, dl0, dr0)

    dots(STEPS - 2, dl0, dr0)
    scores(STEPS - 3, dl1, dr1)
    send_rows((6,))
    dots(STEPS - 1, dl1, dr1)
    scores(STEPS - 2, dl0, dr0)
    sum_columns(range(12))
    scores(STEPS - 1, dl1, dr1)

    send_rows((7,))

    mine = x * 4 + y
    sum_columns(range(12, 16))

    def col_copy(dx, dy):
        return pltpu.make_async_remote_copy(
            src_ref=col_part.at[dx % 2],
            dst_ref=col_recv.at[mine],
            send_sem=col_sem.at[0],
            recv_sem=col_sem.at[1],
            device_id=device(dx=dx, dy=dy),
            device_id_type=pl.DeviceIdType.MESH,
        )

    plane = [(dx, dy) for dx in range(4) for dy in range(4) if (dx, dy) != (0, 0)]
    for dx, dy in sorted(plane, key=lambda d: -(min(d[0], 4 - d[0]) + min(d[1], 4 - d[1]))):
        col_copy(dx, dy).start()
    col_recv[mine] = col_part[0]
    row_recv[0] = row_part[0]

    all_of(row_recv.at[pl.ds(0, 31)], row_sem.at[1])
    line = row_recv[0]
    for number in range(1, 32):
        line = line + row_recv[number]
    row_out[...] = jnp.where(core == 0, line[:, :64], line[:, 64:])
    all_of(col_recv.at[pl.ds(0, 15)], col_sem.at[1])
    def summed(senders, place):
        return functools.reduce(lambda s, t: s + t, [col_recv[n, place] for n in senders])[:, :HALF]

    parts = []
    for g in range(8):
        x_hi, yy = g // 4, g % 4
        parts.append(summed([(2 * x_hi + a) * 4 + b for a in range(2) for b in range(4)], yy))
        parts.append(summed([a * 4 + yy // 2 * 2 + b for a in range(4) for b in range(2)], 4 + x_hi * 2 + yy % 2))
    for q in range(4):
        a, b, c, d = parts[4 * q : 4 * q + 4]
        col_out[3 * q : 3 * q + 1, :] = jnp.concatenate([a, b[:, :32]], axis=1)
        col_out[3 * q + 1 : 3 * q + 2, :] = jnp.concatenate([b[:, 32:], c[:, :64]], axis=1)
        col_out[3 * q + 2 : 3 * q + 3, :] = jnp.concatenate([c[:, 64:], d], axis=1)

    all_of(tb.at[:, pl.ds(0, 14 * HALF), :], send_sem.at[0])
    all_of(ib.at[:, pl.ds(0, 31 * 64), :], send_sem.at[1])
    all_of(bc.at[0, 0, pl.ds(0, 72), :], send_sem.at[2])
    all_of(row_recv.at[pl.ds(0, 31)], row_sem.at[0])
    all_of(col_recv.at[pl.ds(0, 15)], col_sem.at[0])


def shards(
    image_learn,
    image_refer,
    text_learn,
    text_refer,
    image_scale_learn,
    image_scale_refer,
    text_scale_learn,
    text_scale_refer,
    pair_index,
):
    offset = math.log(text_scale_learn.shape[0] * lax.axis_size("col"))
    vmem, dma = pltpu.VMEM, pltpu.SemaphoreType.DMA
    in_hbm = pl.BlockSpec(memory_space=pltpu.HBM)
    rows, cols = pl.pallas_call(
        functools.partial(kernel, (1.0 - offset) * LOG2E, (-1.0 - offset) * LOG2E),
        out_shape=[jax.ShapeDtypeStruct((1, 64), F32), jax.ShapeDtypeStruct((12, 128), F32)],
        in_specs=[in_hbm] * 9,
        out_specs=[pl.BlockSpec(memory_space=vmem)] * 2,
        scratch_shapes=[
            vmem((2, 4 * CHUNK, E), jnp.bfloat16),
            vmem((2, 8 * BLOCK, E), jnp.bfloat16),
            vmem((2, 2, 16, 128), F32),
            vmem((2, 16, 128), jnp.int32),
            vmem((2, 2, 12, 128), F32),
            vmem((2, 2, 1536, 128), F32),
            vmem((2, 4 * CHUNK, 128), F32),
            vmem((8, 8, BLOCK), F32),
            vmem((8, 8, BLOCK), jnp.int32),
            pltpu.SMEM((16,), jnp.int32),
            vmem((8, 8, BLOCK), F32),
            vmem((4 * CHUNK, 128), F32),
            vmem((CHUNK, BLOCK), F32),
            vmem((CHUNK, BLOCK), F32),
            vmem((CHUNK, BLOCK), F32),
            vmem((CHUNK, BLOCK), F32),
            vmem((16, 1, 128), F32),
            vmem((32, 1, 128), F32),
            vmem((2, 8, 1, 128), F32),
            vmem((16, 8, 1, 128), F32),
            dma((5,)),
            dma((3,)),
            dma((28,)),
            dma((2,)),
            dma((2,)),
            pltpu.SemaphoreType.REGULAR((3,)),
        ],
        compiler_params=pltpu.CompilerParams(
            collective_id=0, has_side_effects=True, vmem_limit_bytes=60 * 2**20
        ),
        cost_estimate=pl.CostEstimate(
            flops=4 * 2048 * 1536 * E, bytes_accessed=2**21, transcendentals=3 * 2048 * 1536
        ),
        name="gather_score",
    )(
        image_learn,
        image_refer,
        text_learn,
        text_refer,
        image_scale_learn.reshape(16, 128),
        image_scale_refer.reshape(16, 128),
        text_scale_learn.reshape(12, 128),
        text_scale_refer.reshape(12, 128),
        pair_index.reshape(16, 128),
    )
    return rows.reshape(64), cols.reshape(1536)


def solution(mesh):
    in_specs = (
        P(("grp", "col"), None),
        P(("grp", "col"), None),
        P("col", "grp", None),
        P("col", "grp", None),
        P("grp"),
        P("grp"),
        P("col"),
        P("col"),
        P("grp"),
    )
    out_specs = (P(("grp", "col")), P("col"))
    return jax.shard_map(shards, mesh=mesh, in_specs=in_specs, out_specs=out_specs, check_vma=False)
```

```python
import functools
import math

import jax
import jax.numpy as jnp
from jax import lax
from jax.experimental import pallas as pl
from jax.experimental.pallas import tpu as pltpu
from jax.sharding import PartitionSpec as P

F32 = jnp.float32
LOG2E = 1.0 / math.log(2.0)
LN2 = math.log(2.0)
SERIES = tuple(2.0 * LOG2E * c for c in (0.99999984, 0.33337989, 0.1979503, 0.17111227))

E = 1152
HALF = 96
CHUNK = 4 * HALF
SPLIT = {1: 1024, 2: 1024, 3: 1024, 4: 1024}
BLOCK = 256
PIECE_Z = (0, 0, 1, -1, 1, -1, 2, -2, 2, -2, 3, -3, 3, -3, 4, 4)
PIECE_LANE = (0, 1, 0, 0, 1, 1, 0, 0, 1, 1, 0, 0, 1, 1, 0, 1)
STEPS = 32
VMEM_GRANT = 56539217


def wrap(value, size):
    return lax.rem(value + size, size)


def score(dot_learn, dot_refer, a_learn, a_refer, b_learn, b_refer, paired, c_learn, c_refer):
    u = dot_learn * a_learn * b_learn + c_learn
    w = dot_refer * a_refer * b_refer + c_refer
    p = jnp.exp2(-jnp.abs(u))
    q = jnp.exp2(-jnp.abs(w))
    z = (p - q) * pl.reciprocal((p + q) + 2.0, approx=True)
    s = z * z
    poly = s * SERIES[3] + SERIES[2]
    poly = poly * s + SERIES[1]
    poly = poly * s + SERIES[0]
    d = (jnp.maximum(u, 0.0) - jnp.maximum(w, 0.0)) + z * poly
    return d - jnp.where(paired, u - w, 0.0)


def kernel(
    c_learn,
    c_refer,
    img_l,
    img_r,
    txt_l,
    txt_r,
    isc_l,
    isc_r,
    tsc_l,
    tsc_r,
    pair,
    row_out,
    col_out,
    tb,
    ib,
    isc,
    ipr,
    tsc,
    bc,
    tcol,
    irow,
    iprow,
    base,
    rs,
    cs,
    dl0,
    dr0,
    dl1,
    dr1,
    row_part,
    row_recv,
    col_part,
    col_recv,
    local_sem,
    send_sem,
    recv_sem,
    row_sem,
    col_sem,
    ready,
):
    grp, col = lax.axis_index("grp"), lax.axis_index("col")
    x = lax.div(grp, 4) * 2 + lax.rem(lax.div(col, 2), 2)
    y = lax.rem(grp, 4)
    z = lax.div(col, 4)
    core = lax.rem(col, 2)
    x_odd, y_odd = lax.rem(x, 2), lax.rem(y, 2)
    x_pair, y_pair = x + 1 - 2 * x_odd, y + 1 - 2 * y_odd
    x_diag, y_diag = wrap(x - 1 + 2 * x_odd, 4), wrap(y - 1 + 2 * y_odd, 4)

    def device(dx=0, dy=0, dz=0, at_x=None, at_y=None, at_core=None):
        px = wrap(x + dx, 4) if at_x is None else at_x
        py = wrap(y + dy, 4) if at_y is None else at_y
        pz = wrap(z + dz, 8)
        pc = core if at_core is None else at_core
        return lax.div(px, 2) * 4 + py, (pz * 2 + lax.rem(px, 2)) * 2 + pc

    other_core = device(at_core=1 - core)
    diag = device(at_x=x_diag, at_y=y_diag)
    pair_x, next_x = device(at_x=x_pair), device(at_x=x_diag)
    pair_y, next_y = device(at_y=y_pair), device(at_y=y_diag)
    up_z, dn_z = device(dz=1), device(dz=-1)

    groups, messages = {}, {}

    def group(name, ref):
        groups[name] = (len(groups), ref)

    def message(name, group_name, copies, to):
        messages[name] = (group_name, copies, to)

    def text(piece, start=0, rows=HALF):
        return tb.at[:, pl.ds(piece * HALF + start, rows), :]

    def image(piece, part=None, first=0, size=E):
        rows = 64 if part is None else 32
        off = piece * 128 + core * 64 + (0 if part is None else part * 32)
        return ib.at[:, pl.ds(pl.multiple_of(off, 32), rows), pl.ds(first, size)]

    group("scales", bc.at[0, 0, pl.ds(0, 72), :])
    message("tsc", "scales", [(tsc_l, tsc.at[1, 0]), (tsc_r, tsc.at[1, 1])], pair_x)
    message("isc", "scales", [(isc_l, isc.at[1, 0]), (isc_r, isc.at[1, 1]), (pair, ipr.at[1])], diag)
    group("tp", tb.at[:, pl.ds(0, 192), :])
    first, second = pl.ds(0, HALF), pl.ds(HALF, HALF)
    message("t1p", "tp", [(t.at[0, first, :], text(2).at[i]) for i, t in enumerate((txt_l, txt_r))], pair_x)
    message("t2p", "tp", [(t.at[0, second, :], text(3).at[i]) for i, t in enumerate((txt_l, txt_r))], pair_y)
    group("ip", ib.at[:, pl.ds(0, 64), :])
    message("ip", "ip", [(r, image(1).at[i]) for i, r in enumerate((img_l, img_r))], diag)
    for name in ("oP", "oN", "qP", "qN"):
        group("t" + name, tb.at[:, pl.ds(0, 192), :])
    group("t2", tb.at[:, pl.ds(0, 384), :])
    for name, first, to_p, to_n in (("t1", 0, pair_y, next_y), ("t2", 1, pair_x, next_x)):
        o, far = 4 + 2 * first, 12 + first
        message(name + "oP", "toP", [(text(first), text(o))], to_p)
        for part, start_row, rows in (("a", 0, 32), ("b", 32, 64)):
            message(name + "oN" + part, "toN", [(text(first, start_row, rows), text(o + 1, start_row, rows))], to_n)
        message(name + "qP", "tqP", [(text(2 + first), text(o + 4))], to_p)
        for part, start_row in (("a", 0), ("b", 48)):
            message(name + "qN" + part, "tqN", [(text(2 + first, start_row, 48), text(o + 5, start_row, 48))], to_n)
        message(name + "o2A", "t2", [(text(o, 0, 48), text(far, 0, 48))], to_n)
        message(name + "o2B", "t2", [(text(o + 1, 48, 48), text(far, 48, 48))], to_p)
        message(name + "q2A", "t2", [(text(o + 4, 0, 48), text(far + 2, 0, 48))], to_n)
        message(name + "q2B", "t2", [(text(o + 5, 48, 48), text(far + 2, 48, 48))], to_p)
    for lane, mark in ((0, "o"), (1, "q")):
        place = {dz: p for p, dz in enumerate(PIECE_Z) if PIECE_LANE[p] == lane}
        for k in (1, 2, 3, 4):
            size = E if lane == 0 else SPLIT[k]
            ring = f"i{mark}{k}"
            if ring != "io1":
                group(ring, ib.at[:, pl.ds(0, 128 if k < 4 else 64), pl.ds(0, size)])
            if ring in ("io1", "io2"):
                for i, (part, own) in enumerate((("l", img_l), ("r", img_r))):
                    if ring == "io1":
                        group(ring + part, ib.at[0, pl.ds(0, 128), :])
                    for sign, to, at in (("+", dn_z, 1), ("-", up_z, -1)):
                        src = own if ring == "io1" else image(place[at]).at[i]
                        group_name = ring + part if ring == "io1" else ring
                        message(ring + part + sign, group_name, [(src, image(place[k * at]).at[i])], to)
            elif k < 4:
                message(ring + "+", ring, [(image(place[k - 1], size=size), image(place[k], size=size))], dn_z)
                message(ring + "-", ring, [(image(place[1 - k], size=size), image(place[-k], size=size))], up_z)
            else:
                message(ring + "+", ring, [(image(place[3], 0, size=size), image(place[4], 0, size=size))], dn_z)
                message(ring + "-", ring, [(image(place[-3], 1, size=size), image(place[4], 1, size=size))], up_z)
            if lane == 0 and SPLIT[k] < E:
                rest = dict(first=SPLIT[k], size=E - SPLIT[k])
                group(f"x{k}", ib.at[:, pl.ds(0, 128 if k < 4 else 64), pl.ds(0, E - SPLIT[k])])
                for at in (k, -k) if k < 4 else (k,):
                    there = [p for p in range(16) if PIECE_Z[p] == at and PIECE_LANE[p] == 1][0]
                    message(f"x{k}{at}", f"x{k}", [(image(place[at], **rest), image(there, **rest))], diag)
    for block in range(8):
        if block != 1:
            group(f"s{block}", ib.at[:, pl.ds(0, 128 if block else 256), :])
    for piece in range(16):
        message(f"s{piece}", f"s{piece // 2 if piece > 3 else 0}", [(image(piece), image(piece))], other_core)

    def sender(name):
        return 2 if name in ("tsc", "isc") else 0 if name[0] == "t" else 1

    def start(*names):
        for name in names:
            group_name, copies, to = messages[name]
            for src, dst in copies:
                pltpu.make_async_remote_copy(
                    src_ref=src,
                    dst_ref=dst,
                    send_sem=send_sem.at[sender(name)],
                    recv_sem=recv_sem.at[groups[group_name][0]],
                    device_id=to,
                    device_id_type=pl.DeviceIdType.MESH,
                ).start()

    def all_of(ref, sem):
        pltpu.make_async_copy(ref, ref, sem).wait()

    def got(*names):
        for name in names:
            number, ref = groups[name]
            all_of(ref, recv_sem.at[number])

    own_rows = pl.ds(pl.multiple_of(core * 64, 64), 64)
    barrier = pltpu.get_barrier_semaphore()
    near = (pair_x, next_x, pair_y, next_y)
    for to in near + (up_z, dn_z, other_core, diag):
        pl.semaphore_signal(barrier, inc=1, device_id=to, device_id_type=pl.DeviceIdType.MESH)
    loads = [
        (0, txt_l.at[0], tb.at[0, pl.ds(0, 2 * HALF), :]),
        (0, txt_r.at[0], tb.at[1, pl.ds(0, 2 * HALF), :]),
        (1, img_l, ib.at[0, own_rows, :]),
        (1, img_r, ib.at[1, own_rows, :]),
        (2, isc_l, isc.at[0, 0]),
        (2, isc_r, isc.at[0, 1]),
        (3, tsc_l, tsc.at[0, 0]),
        (3, tsc_r, tsc.at[0, 1]),
        (4, pair, ipr.at[0]),
    ]
    for number, src, dst in loads:
        pltpu.make_async_copy(src, dst, local_sem.at[number]).start()

    pl.semaphore_wait(barrier, 8)
    start("tsc", "isc", "ip", "t1p", "t2p", "io1l+", "io1l-", "io1r+", "io1r-")
    for number, ref in enumerate((tb.at[:, pl.ds(0, 2 * HALF), :], ib.at[:, own_rows, :], isc.at[0], tsc.at[0], ipr.at[0])):
        all_of(ref, local_sem.at[number])
    start("s0", "t1oNa", "t2oNa", "t2oNb", "t1oP", "t2oP")

    def tell(r):
        for to in near:
            pl.semaphore_signal(ready.at[r], inc=1, device_id=to, device_id_type=pl.DeviceIdType.MESH)

    def told(r):
        pl.semaphore_wait(ready.at[r], 4)

    tell(0)

    def source(piece):
        if piece < 4:
            lane, half, side = piece // 2, piece % 2, 0
        elif piece < 12:
            lane, half, side = (piece - 4) // 4, ((piece - 4) // 2) % 2, 1 + piece % 2
        else:
            lane, half, side = (piece - 12) // 2, piece % 2, 3
        along_x, along_y = (x, x_pair, x_diag, wrap(x + 2, 4)), (y, y_pair, y_diag, wrap(y + 2, 4))
        px = along_x[side] if half == 1 else along_x[lane]
        py = along_y[side] if half == 0 else along_y[lane]
        same = lane == 0 if half == 0 else side in (0, 3)
        return px, py, half, same

    def spread(which):
        @pl.loop(0, 24)
        def _(i):
            k, q = lax.div(i, 12), lax.rem(i, 12)
            line = tsc[which, k, pl.ds(q, 1), :]
            bc[which, k, pl.ds(pl.multiple_of(q * 128, 128), 128), :] = jnp.transpose(
                jnp.broadcast_to(line, (128, 128))
            )

    def text_setup(which):
        for piece in range(16):
            px, py, half, same = source(piece)
            if same != (which == 0):
                continue
            off = (lax.div(px, 2) * 4 + py) * 192 + half * HALF
            block = (z * 2 + lax.rem(px, 2)) * 2 + core
            base[piece] = block * 1536 + off
            for k in range(2):
                tcol[k, pl.ds(piece * HALF, HALF), :] = bc[which, k, pl.ds(pl.multiple_of(off, 32), HALF), :]

    def image_setup(lane):
        odd = x_odd if lane == 0 else 1 - x_odd
        for piece in range(16):
            if PIECE_LANE[piece] != lane:
                continue
            block, lanes = piece // 2, pl.ds((piece % 2) * 128, 128)
            at = pl.ds(wrap(z + PIECE_Z[piece], 8) * 2 + odd, 1)
            irow[block, 0:1, lanes] = isc[lane, 0, at, :] * (4.0 * LOG2E)
            irow[block, 1:2, lanes] = isc[lane, 1, at, :] * (6.0 * LOG2E)
            iprow[block, 0:1, lanes] = ipr[lane, at, :]

    def tile(k):
        block = jnp.where(
            k < 18,
            jnp.where(
                k < 8,
                jnp.where(k < 6, lax.rem(k, 3), 3),
                jnp.where(k < 12, k - 8, lax.div(k, 3)),
            ),
            jnp.where(k < 24, jnp.where(k < 22, k - 16, k - 22), lax.div(k, 4)),
        )
        chunk = jnp.where(
            k < 18,
            jnp.where(k < 8, jnp.where(k < 6, lax.div(k, 3), k - 6), jnp.where(k < 12, 2, lax.rem(k, 3))),
            jnp.where(k < 24, 3, lax.rem(k, 4)),
        )
        return block, chunk

    def dots(k, dl, dr):
        block, chunk = tile(k)
        rows = pl.ds(pl.multiple_of(chunk * CHUNK, CHUNK), CHUNK)
        cols = pl.ds(pl.multiple_of(block * BLOCK, BLOCK), BLOCK)
        for which, out in ((0, dl), (1, dr)):
            out[...] = lax.dot_general(
                tb[which, rows, :], ib[which, cols, :], (((1,), (1,)), ((), ())), preferred_element_type=F32
            )

    def scores(k, dl, dr):
        block, chunk = tile(k)
        scale = irow[block]
        a_learn = jnp.broadcast_to(scale[0:1], (8, BLOCK))
        a_refer = jnp.broadcast_to(scale[1:2], (8, BLOCK))
        wanted = jnp.broadcast_to(iprow[block][0:1], (8, BLOCK)) - lax.broadcasted_iota(jnp.int32, (8, BLOCK), 0)
        total = rs[block]
        for piece in range(4):
            here = wanted - base[chunk * 4 + piece]
            for g in range(HALF // 8):
                at = piece * HALF + g * 8
                rows = pl.ds(pl.multiple_of(chunk * CHUNK + at, 8), 8)
                b_learn, b_refer = tcol[0, rows, :], tcol[1, rows, :]
                d = score(
                    dl[at : at + 8, :],
                    dr[at : at + 8, :],
                    a_learn,
                    a_refer,
                    jnp.concatenate([b_learn, b_learn], axis=1),
                    jnp.concatenate([b_refer, b_refer], axis=1),
                    here == g * 8,
                    c_learn,
                    c_refer,
                )
                total = total + d
                cs[rows, :] = cs[rows, :] + (d[:, :128] + d[:, 128:])
        rs[block] = total

    rs[...] = jnp.zeros_like(rs)
    cs[...] = jnp.zeros_like(cs)
    spread(0)
    text_setup(0)
    image_setup(0)

    def row_copy(piece, which):
        number = piece * 2 + which
        at_core = core if which == 0 else 1 - core
        if PIECE_LANE[piece] == 0:
            to = device(dz=PIECE_Z[piece], at_core=at_core)
        else:
            to = device(dz=PIECE_Z[piece], at_x=x_diag, at_y=y_diag, at_core=at_core)
        return pltpu.make_async_remote_copy(
            src_ref=row_part.at[piece],
            dst_ref=row_recv.at[number],
            send_sem=row_sem.at[0],
            recv_sem=row_sem.at[1],
            device_id=to,
            device_id_type=pl.DeviceIdType.MESH,
        )

    row_messages = [(piece, which) for piece in range(16) for which in range(2) if (piece, which) != (0, 0)]

    def send_rows(blocks):
        for block in blocks:
            line = jnp.sum(rs[block], axis=0, keepdims=True) * LN2
            row_part[block * 2] = line[:, :128]
            row_part[block * 2 + 1] = line[:, 128:]
        for piece, which in reversed(row_messages):
            if piece // 2 in blocks:
                row_copy(piece, which).start()

    def sum_columns(pieces):
        for piece in pieces:
            px, py, half, same = source(piece)
            line = jnp.sum(jnp.transpose(cs[pl.ds(piece * HALF, HALF), :]), axis=0, keepdims=True) * LN2
            place = py if half == 0 else 4 + lax.div(px, 2) * 2 + lax.rem(py, 2)
            col_part[0 if same else 1, place, :, 0:HALF] = line

    got("scales")
    spread(1)
    got("io1l")
    start("io2l+", "io2l-")
    text_setup(1)
    image_setup(1)
    got("io1r")
    start("x11", "x1-1", "s2", "s3")
    got("ip")
    start("iq1+", "iq1-", "io2r+", "io2r-", "s1", "t1oNb")
    told(0)
    tell(1)
    got("tp")
    start("t1qP", "t2qP", "t1qNa", "t2qNa")
    got("s0")

    def events(i):
        if i == 1:
            got("iq1")
            start("iq2+", "iq2-")
            got("x1")
            start("s4", "s5")
            got("toN")
            start("t1o2B", "t2o2B")
            got("io2")
            start("x22", "x2-2", "t1qNb", "t2qNb", "io3+", "io3-", "s6", "s7")
            got("toP")
            start("t1o2A", "t2o2A")
            got("s2")
        elif i == 3:
            got("s3")
            told(1)
            tell(2)
        elif i == 4:
            got("iq2")
            start("iq3+", "iq3-")
            got("x2")
            start("s8", "s9")
            got("tqN")
            start("t1q2B", "t2q2B")
            got("tqP")
            start("t1q2A", "t2q2A")
        elif i == 5:
            got("io3")
            start("io4+", "io4-", "s10", "s11", "x33", "x3-3")
        elif i == 6:
            got("s4")
        elif i == 7:
            got("s5")
        elif i == 9:
            got("iq3")
            start("iq4+", "iq4-")
            got("t2")
        elif i == 10:
            got("io4")
            start("x44", "s14")
        elif i == 11:
            got("x3")
            start("s12", "s13")
        elif i == 12:
            told(2)
            send_rows((0, 2, 3, 4, 5))
            got("s6")
        elif i == 13:
            got("iq4", "x4")
            start("s15")
        elif i == 14:
            send_rows((1,))
            got("s7")

    dots(0, dl0, dr0)
    dots(1, dl1, dr1)
    scores(0, dl0, dr0)

    @pl.loop(1, STEPS // 2 - 1)
    def _(i):
        for low, high in ((1, 4), (4, 10), (10, 15)):

            @pl.when((i >= low) & (i < high))
            def _(low=low, high=high):
                for at in range(low, high):
                    if at not in (2, 8):

                        @pl.when(i == at)
                        def _(at=at):
                            events(at)

        dots(2 * i, dl0, dr0)
        scores(2 * i - 1, dl1, dr1)
        dots(2 * i + 1, dl1, dr1)
        scores(2 * i, dl0, dr0)

    dots(STEPS - 2, dl0, dr0)
    scores(STEPS - 3, dl1, dr1)
    send_rows((6,))
    dots(STEPS - 1, dl1, dr1)
    scores(STEPS - 2, dl0, dr0)
    sum_columns(range(12))
    scores(STEPS - 1, dl1, dr1)

    send_rows((7,))

    mine = x * 4 + y
    sum_columns(range(12, 16))

    def col_copy(dx, dy):
        return pltpu.make_async_remote_copy(
            src_ref=col_part.at[dx % 2],
            dst_ref=col_recv.at[mine],
            send_sem=col_sem.at[0],
            recv_sem=col_sem.at[1],
            device_id=device(dx=dx, dy=dy),
            device_id_type=pl.DeviceIdType.MESH,
        )

    plane = [(dx, dy) for dx in range(4) for dy in range(4) if (dx, dy) != (0, 0)]
    for dx, dy in sorted(plane, key=lambda d: -(min(d[0], 4 - d[0]) + min(d[1], 4 - d[1]))):
        col_copy(dx, dy).start()
    col_recv[mine] = col_part[0]
    row_recv[0] = row_part[0]

    all_of(row_recv.at[pl.ds(0, 31)], row_sem.at[1])
    line = row_recv[0]
    for number in range(1, 32):
        line = line + row_recv[number]
    row_out[...] = jnp.where(core == 0, line[:, :64], line[:, 64:])
    all_of(col_recv.at[pl.ds(0, 15)], col_sem.at[1])
    def summed(senders, place):
        return functools.reduce(lambda s, t: s + t, [col_recv[n, place] for n in senders])[:, :HALF]

    parts = []
    for g in range(8):
        x_hi, yy = g // 4, g % 4
        parts.append(summed([(2 * x_hi + a) * 4 + b for a in range(2) for b in range(4)], yy))
        parts.append(summed([a * 4 + yy // 2 * 2 + b for a in range(4) for b in range(2)], 4 + x_hi * 2 + yy % 2))
    for q in range(4):
        a, b, c, d = parts[4 * q : 4 * q + 4]
        col_out[3 * q : 3 * q + 1, :] = jnp.concatenate([a, b[:, :32]], axis=1)
        col_out[3 * q + 1 : 3 * q + 2, :] = jnp.concatenate([b[:, 32:], c[:, :64]], axis=1)
        col_out[3 * q + 2 : 3 * q + 3, :] = jnp.concatenate([c[:, 64:], d], axis=1)

    all_of(tb.at[:, pl.ds(0, 14 * HALF), :], send_sem.at[0])
    all_of(ib.at[:, pl.ds(0, 31 * 64), :], send_sem.at[1])
    all_of(bc.at[0, 0, pl.ds(0, 72), :], send_sem.at[2])
    all_of(row_recv.at[pl.ds(0, 31)], row_sem.at[0])
    all_of(col_recv.at[pl.ds(0, 15)], col_sem.at[0])


def shards(
    image_learn,
    image_refer,
    text_learn,
    text_refer,
    image_scale_learn,
    image_scale_refer,
    text_scale_learn,
    text_scale_refer,
    pair_index,
):
    offset = math.log(text_scale_learn.shape[0] * lax.axis_size("col"))
    vmem, dma = pltpu.VMEM, pltpu.SemaphoreType.DMA
    in_hbm = pl.BlockSpec(memory_space=pltpu.HBM)
    rows, cols = pl.pallas_call(
        functools.partial(kernel, (1.0 - offset) * LOG2E, (-1.0 - offset) * LOG2E),
        out_shape=[jax.ShapeDtypeStruct((1, 64), F32), jax.ShapeDtypeStruct((12, 128), F32)],
        in_specs=[in_hbm] * 9,
        out_specs=[pl.BlockSpec(memory_space=vmem)] * 2,
        scratch_shapes=[
            vmem((2, 4 * CHUNK, E), jnp.bfloat16),
            vmem((2, 8 * BLOCK, E), jnp.bfloat16),
            vmem((2, 2, 16, 128), F32),
            vmem((2, 16, 128), jnp.int32),
            vmem((2, 2, 12, 128), F32),
            vmem((2, 2, 1536, 128), F32),
            vmem((2, 4 * CHUNK, 128), F32),
            vmem((8, 8, BLOCK), F32),
            vmem((8, 8, BLOCK), jnp.int32),
            pltpu.SMEM((16,), jnp.int32),
            vmem((8, 8, BLOCK), F32),
            vmem((4 * CHUNK, 128), F32),
            vmem((CHUNK, BLOCK), F32),
            vmem((CHUNK, BLOCK), F32),
            vmem((CHUNK, BLOCK), F32),
            vmem((CHUNK, BLOCK), F32),
            vmem((16, 1, 128), F32),
            vmem((32, 1, 128), F32),
            vmem((2, 8, 1, 128), F32),
            vmem((16, 8, 1, 128), F32),
            dma((5,)),
            dma((3,)),
            dma((28,)),
            dma((2,)),
            dma((2,)),
            pltpu.SemaphoreType.REGULAR((3,)),
        ],
        compiler_params=pltpu.CompilerParams(
            collective_id=0, has_side_effects=True, vmem_limit_bytes=VMEM_GRANT
        ),
        cost_estimate=pl.CostEstimate(
            flops=4 * 2048 * 1536 * E, bytes_accessed=2**21, transcendentals=3 * 2048 * 1536
        ),
        name="gather_score",
    )(
        image_learn,
        image_refer,
        text_learn,
        text_refer,
        image_scale_learn.reshape(16, 128),
        image_scale_refer.reshape(16, 128),
        text_scale_learn.reshape(12, 128),
        text_scale_refer.reshape(12, 128),
        pair_index.reshape(16, 128),
    )
    return rows.reshape(64), cols.reshape(1536)


def solution(mesh):
    in_specs = (
        P(("grp", "col"), None),
        P(("grp", "col"), None),
        P("col", "grp", None),
        P("col", "grp", None),
        P("grp"),
        P("grp"),
        P("col"),
        P("col"),
        P("grp"),
    )
    out_specs = (P(("grp", "col")), P("col"))
    return jax.shard_map(shards, mesh=mesh, in_specs=in_specs, out_specs=out_specs, check_vma=False)
```

```python
import functools
import math

import jax
import jax.numpy as jnp
from jax import lax
from jax.experimental import pallas as pl
from jax.experimental.pallas import tpu as pltpu
from jax.sharding import PartitionSpec as P

F32 = jnp.float32
LOG2E = 1.0 / math.log(2.0)
LN2 = math.log(2.0)
SERIES = tuple(2.0 * LOG2E * c for c in (0.99999984, 0.33337989, 0.1979503, 0.17111227))

E = 1152
HALF = 96
CHUNK = 4 * HALF
SPLIT = {1: 1024, 2: 1024, 3: 1024, 4: 896}
BLOCK = 256
PIECE_Z = (0, 0, 1, -1, 1, -1, 2, -2, 2, -2, 3, -3, 3, -3, 4, 4)
PIECE_LANE = (0, 1, 0, 0, 1, 1, 0, 0, 1, 1, 0, 0, 1, 1, 0, 1)
STEPS = 32
VMEM_GRANT = 56539217


def wrap(value, size):
    return lax.rem(value + size, size)


def score(dot_learn, dot_refer, a_learn, a_refer, b_learn, b_refer, paired, c_learn, c_refer):
    u = dot_learn * a_learn * b_learn + c_learn
    w = dot_refer * a_refer * b_refer + c_refer
    p = jnp.exp2(-jnp.abs(u))
    q = jnp.exp2(-jnp.abs(w))
    z = (p - q) * pl.reciprocal((p + q) + 2.0, approx=True)
    s = z * z
    poly = s * SERIES[3] + SERIES[2]
    poly = poly * s + SERIES[1]
    poly = poly * s + SERIES[0]
    d = (jnp.maximum(u, 0.0) - jnp.maximum(w, 0.0)) + z * poly
    return d - jnp.where(paired, u - w, 0.0)


def kernel(
    c_learn,
    c_refer,
    img_l,
    img_r,
    txt_l,
    txt_r,
    isc_l,
    isc_r,
    tsc_l,
    tsc_r,
    pair,
    row_out,
    col_out,
    tb,
    ib,
    isc,
    ipr,
    tsc,
    bc,
    tcol,
    irow,
    iprow,
    base,
    rs,
    cs,
    dl0,
    dr0,
    dl1,
    dr1,
    row_part,
    row_recv,
    col_part,
    col_recv,
    local_sem,
    send_sem,
    recv_sem,
    row_sem,
    col_sem,
    ready,
):
    grp, col = lax.axis_index("grp"), lax.axis_index("col")
    x = lax.div(grp, 4) * 2 + lax.rem(lax.div(col, 2), 2)
    y = lax.rem(grp, 4)
    z = lax.div(col, 4)
    core = lax.rem(col, 2)
    x_odd, y_odd = lax.rem(x, 2), lax.rem(y, 2)
    x_pair, y_pair = x + 1 - 2 * x_odd, y + 1 - 2 * y_odd
    x_diag, y_diag = wrap(x - 1 + 2 * x_odd, 4), wrap(y - 1 + 2 * y_odd, 4)

    def device(dx=0, dy=0, dz=0, at_x=None, at_y=None, at_core=None):
        px = wrap(x + dx, 4) if at_x is None else at_x
        py = wrap(y + dy, 4) if at_y is None else at_y
        pz = wrap(z + dz, 8)
        pc = core if at_core is None else at_core
        return lax.div(px, 2) * 4 + py, (pz * 2 + lax.rem(px, 2)) * 2 + pc

    other_core = device(at_core=1 - core)
    diag = device(at_x=x_diag, at_y=y_diag)
    pair_x, next_x = device(at_x=x_pair), device(at_x=x_diag)
    pair_y, next_y = device(at_y=y_pair), device(at_y=y_diag)
    up_z, dn_z = device(dz=1), device(dz=-1)

    groups, messages = {}, {}

    def group(name, ref):
        groups[name] = (len(groups), ref)

    def message(name, group_name, copies, to):
        messages[name] = (group_name, copies, to)

    def text(piece, start=0, rows=HALF):
        return tb.at[:, pl.ds(piece * HALF + start, rows), :]

    def image(piece, part=None, first=0, size=E):
        rows = 64 if part is None else 32
        off = piece * 128 + core * 64 + (0 if part is None else part * 32)
        return ib.at[:, pl.ds(pl.multiple_of(off, 32), rows), pl.ds(first, size)]

    group("scales", bc.at[0, 0, pl.ds(0, 72), :])
    message("tsc", "scales", [(tsc_l, tsc.at[1, 0]), (tsc_r, tsc.at[1, 1])], pair_x)
    message("isc", "scales", [(isc_l, isc.at[1, 0]), (isc_r, isc.at[1, 1]), (pair, ipr.at[1])], diag)
    group("tp", tb.at[:, pl.ds(0, 192), :])
    first, second = pl.ds(0, HALF), pl.ds(HALF, HALF)
    message("t1p", "tp", [(t.at[0, first, :], text(2).at[i]) for i, t in enumerate((txt_l, txt_r))], pair_x)
    message("t2p", "tp", [(t.at[0, second, :], text(3).at[i]) for i, t in enumerate((txt_l, txt_r))], pair_y)
    group("ip", ib.at[:, pl.ds(0, 64), :])
    message("ip", "ip", [(r, image(1).at[i]) for i, r in enumerate((img_l, img_r))], diag)
    for name in ("oP", "oN", "qP", "qN"):
        group("t" + name, tb.at[:, pl.ds(0, 192), :])
    group("t2", tb.at[:, pl.ds(0, 384), :])
    for name, first, to_p, to_n in (("t1", 0, pair_y, next_y), ("t2", 1, pair_x, next_x)):
        o, far = 4 + 2 * first, 12 + first
        message(name + "oP", "toP", [(text(first), text(o))], to_p)
        for part, start_row, rows in (("a", 0, 64), ("b", 64, 32)):
            message(name + "oN" + part, "toN", [(text(first, start_row, rows), text(o + 1, start_row, rows))], to_n)
        message(name + "qP", "tqP", [(text(2 + first), text(o + 4))], to_p)
        for part, start_row in (("a", 0), ("b", 48)):
            message(name + "qN" + part, "tqN", [(text(2 + first, start_row, 48), text(o + 5, start_row, 48))], to_n)
        message(name + "o2A", "t2", [(text(o, 0, 48), text(far, 0, 48))], to_n)
        message(name + "o2B", "t2", [(text(o + 1, 48, 48), text(far, 48, 48))], to_p)
        message(name + "q2A", "t2", [(text(o + 4, 0, 48), text(far + 2, 0, 48))], to_n)
        message(name + "q2B", "t2", [(text(o + 5, 48, 48), text(far + 2, 48, 48))], to_p)
    for lane, mark in ((0, "o"), (1, "q")):
        place = {dz: p for p, dz in enumerate(PIECE_Z) if PIECE_LANE[p] == lane}
        for k in (1, 2, 3, 4):
            size = E if lane == 0 else SPLIT[k]
            ring = f"i{mark}{k}"
            if ring != "io1":
                group(ring, ib.at[:, pl.ds(0, 128 if k < 4 else 64), pl.ds(0, size)])
            if ring in ("io1", "io2"):
                for i, (part, own) in enumerate((("l", img_l), ("r", img_r))):
                    if ring == "io1":
                        group(ring + part, ib.at[0, pl.ds(0, 128), :])
                    for sign, to, at in (("+", dn_z, 1), ("-", up_z, -1)):
                        src = own if ring == "io1" else image(place[at]).at[i]
                        group_name = ring + part if ring == "io1" else ring
                        message(ring + part + sign, group_name, [(src, image(place[k * at]).at[i])], to)
            elif k < 4:
                message(ring + "+", ring, [(image(place[k - 1], size=size), image(place[k], size=size))], dn_z)
                message(ring + "-", ring, [(image(place[1 - k], size=size), image(place[-k], size=size))], up_z)
            else:
                message(ring + "+", ring, [(image(place[3], 0, size=size), image(place[4], 0, size=size))], dn_z)
                message(ring + "-", ring, [(image(place[-3], 1, size=size), image(place[4], 1, size=size))], up_z)
            if lane == 0 and SPLIT[k] < E:
                rest = dict(first=SPLIT[k], size=E - SPLIT[k])
                group(f"x{k}", ib.at[:, pl.ds(0, 128 if k < 4 else 64), pl.ds(0, E - SPLIT[k])])
                for at in (k, -k) if k < 4 else (k,):
                    there = [p for p in range(16) if PIECE_Z[p] == at and PIECE_LANE[p] == 1][0]
                    message(f"x{k}{at}", f"x{k}", [(image(place[at], **rest), image(there, **rest))], diag)
    for block in range(8):
        if block != 1:
            group(f"s{block}", ib.at[:, pl.ds(0, 128 if block else 256), :])
    for piece in range(16):
        message(f"s{piece}", f"s{piece // 2 if piece > 3 else 0}", [(image(piece), image(piece))], other_core)

    def sender(name):
        return 2 if name in ("tsc", "isc") else 0 if name[0] == "t" else 1

    def start(*names):
        for name in names:
            group_name, copies, to = messages[name]
            for src, dst in copies:
                pltpu.make_async_remote_copy(
                    src_ref=src,
                    dst_ref=dst,
                    send_sem=send_sem.at[sender(name)],
                    recv_sem=recv_sem.at[groups[group_name][0]],
                    device_id=to,
                    device_id_type=pl.DeviceIdType.MESH,
                ).start()

    def all_of(ref, sem):
        pltpu.make_async_copy(ref, ref, sem).wait()

    def got(*names):
        for name in names:
            number, ref = groups[name]
            all_of(ref, recv_sem.at[number])

    own_rows = pl.ds(pl.multiple_of(core * 64, 64), 64)
    barrier = pltpu.get_barrier_semaphore()
    near = (pair_x, next_x, pair_y, next_y)
    for to in near + (up_z, dn_z, other_core, diag):
        pl.semaphore_signal(barrier, inc=1, device_id=to, device_id_type=pl.DeviceIdType.MESH)
    loads = [
        (0, txt_l.at[0], tb.at[0, pl.ds(0, 2 * HALF), :]),
        (0, txt_r.at[0], tb.at[1, pl.ds(0, 2 * HALF), :]),
        (1, img_l, ib.at[0, own_rows, :]),
        (1, img_r, ib.at[1, own_rows, :]),
        (2, isc_l, isc.at[0, 0]),
        (2, isc_r, isc.at[0, 1]),
        (3, tsc_l, tsc.at[0, 0]),
        (3, tsc_r, tsc.at[0, 1]),
        (4, pair, ipr.at[0]),
    ]
    for number, src, dst in loads:
        pltpu.make_async_copy(src, dst, local_sem.at[number]).start()

    pl.semaphore_wait(barrier, 8)
    start("tsc", "isc", "ip", "t1p", "t2p", "io1l+", "io1l-", "io1r+", "io1r-")
    for number, ref in enumerate((tb.at[:, pl.ds(0, 2 * HALF), :], ib.at[:, own_rows, :], isc.at[0], tsc.at[0], ipr.at[0])):
        all_of(ref, local_sem.at[number])
    start("s0", "t1oNa", "t2oNa", "t2oNb", "t1oP", "t2oP")

    def tell(r):
        for to in near:
            pl.semaphore_signal(ready.at[r], inc=1, device_id=to, device_id_type=pl.DeviceIdType.MESH)

    def told(r):
        pl.semaphore_wait(ready.at[r], 4)

    tell(0)

    def source(piece):
        if piece < 4:
            lane, half, side = piece // 2, piece % 2, 0
        elif piece < 12:
            lane, half, side = (piece - 4) // 4, ((piece - 4) // 2) % 2, 1 + piece % 2
        else:
            lane, half, side = (piece - 12) // 2, piece % 2, 3
        along_x, along_y = (x, x_pair, x_diag, wrap(x + 2, 4)), (y, y_pair, y_diag, wrap(y + 2, 4))
        px = along_x[side] if half == 1 else along_x[lane]
        py = along_y[side] if half == 0 else along_y[lane]
        same = lane == 0 if half == 0 else side in (0, 3)
        return px, py, half, same

    def spread(which):
        @pl.loop(0, 24)
        def _(i):
            k, q = lax.div(i, 12), lax.rem(i, 12)
            line = tsc[which, k, pl.ds(q, 1), :]
            bc[which, k, pl.ds(pl.multiple_of(q * 128, 128), 128), :] = jnp.transpose(
                jnp.broadcast_to(line, (128, 128))
            )

    def text_setup(which):
        for piece in range(16):
            px, py, half, same = source(piece)
            if same != (which == 0):
                continue
            off = (lax.div(px, 2) * 4 + py) * 192 + half * HALF
            block = (z * 2 + lax.rem(px, 2)) * 2 + core
            base[piece] = block * 1536 + off
            for k in range(2):
                tcol[k, pl.ds(piece * HALF, HALF), :] = bc[which, k, pl.ds(pl.multiple_of(off, 32), HALF), :]

    def image_setup(lane):
        odd = x_odd if lane == 0 else 1 - x_odd
        for piece in range(16):
            if PIECE_LANE[piece] != lane:
                continue
            block, lanes = piece // 2, pl.ds((piece % 2) * 128, 128)
            at = pl.ds(wrap(z + PIECE_Z[piece], 8) * 2 + odd, 1)
            irow[block, 0:1, lanes] = isc[lane, 0, at, :] * (4.0 * LOG2E)
            irow[block, 1:2, lanes] = isc[lane, 1, at, :] * (6.0 * LOG2E)
            iprow[block, 0:1, lanes] = ipr[lane, at, :]

    def tile(k):
        block = jnp.where(
            k < 18,
            jnp.where(
                k < 8,
                jnp.where(k < 6, lax.rem(k, 3), 3),
                jnp.where(k < 12, k - 8, lax.div(k, 3)),
            ),
            jnp.where(k < 24, jnp.where(k < 22, k - 16, k - 22), lax.div(k, 4)),
        )
        chunk = jnp.where(
            k < 18,
            jnp.where(k < 8, jnp.where(k < 6, lax.div(k, 3), k - 6), jnp.where(k < 12, 2, lax.rem(k, 3))),
            jnp.where(k < 24, 3, lax.rem(k, 4)),
        )
        return block, chunk

    def dots(k, dl, dr):
        block, chunk = tile(k)
        rows = pl.ds(pl.multiple_of(chunk * CHUNK, CHUNK), CHUNK)
        cols = pl.ds(pl.multiple_of(block * BLOCK, BLOCK), BLOCK)
        for which, out in ((0, dl), (1, dr)):
            out[...] = lax.dot_general(
                tb[which, rows, :], ib[which, cols, :], (((1,), (1,)), ((), ())), preferred_element_type=F32
            )

    def scores(k, dl, dr):
        block, chunk = tile(k)
        scale = irow[block]
        a_learn = jnp.broadcast_to(scale[0:1], (8, BLOCK))
        a_refer = jnp.broadcast_to(scale[1:2], (8, BLOCK))
        wanted = jnp.broadcast_to(iprow[block][0:1], (8, BLOCK)) - lax.broadcasted_iota(jnp.int32, (8, BLOCK), 0)
        total = rs[block]
        for piece in range(4):
            here = wanted - base[chunk * 4 + piece]
            for g in range(HALF // 8):
                at = piece * HALF + g * 8
                rows = pl.ds(pl.multiple_of(chunk * CHUNK + at, 8), 8)
                b_learn, b_refer = tcol[0, rows, :], tcol[1, rows, :]
                d = score(
                    dl[at : at + 8, :],
                    dr[at : at + 8, :],
                    a_learn,
                    a_refer,
                    jnp.concatenate([b_learn, b_learn], axis=1),
                    jnp.concatenate([b_refer, b_refer], axis=1),
                    here == g * 8,
                    c_learn,
                    c_refer,
                )
                total = total + d
                cs[rows, :] = cs[rows, :] + (d[:, :128] + d[:, 128:])
        rs[block] = total

    rs[...] = jnp.zeros_like(rs)
    cs[...] = jnp.zeros_like(cs)
    spread(0)
    text_setup(0)
    image_setup(0)

    def row_copy(piece, which):
        number = piece * 2 + which
        at_core = core if which == 0 else 1 - core
        if PIECE_LANE[piece] == 0:
            to = device(dz=PIECE_Z[piece], at_core=at_core)
        else:
            to = device(dz=PIECE_Z[piece], at_x=x_diag, at_y=y_diag, at_core=at_core)
        return pltpu.make_async_remote_copy(
            src_ref=row_part.at[piece],
            dst_ref=row_recv.at[number],
            send_sem=row_sem.at[0],
            recv_sem=row_sem.at[1],
            device_id=to,
            device_id_type=pl.DeviceIdType.MESH,
        )

    row_messages = [(piece, which) for piece in range(16) for which in range(2) if (piece, which) != (0, 0)]

    def send_rows(blocks):
        for block in blocks:
            line = jnp.sum(rs[block], axis=0, keepdims=True) * LN2
            row_part[block * 2] = line[:, :128]
            row_part[block * 2 + 1] = line[:, 128:]
        for piece, which in reversed(row_messages):
            if piece // 2 in blocks:
                row_copy(piece, which).start()

    def sum_columns(pieces):
        for piece in pieces:
            px, py, half, same = source(piece)
            line = jnp.sum(jnp.transpose(cs[pl.ds(piece * HALF, HALF), :]), axis=0, keepdims=True) * LN2
            place = py if half == 0 else 4 + lax.div(px, 2) * 2 + lax.rem(py, 2)
            col_part[0 if same else 1, pl.ds(place, 1), 0:HALF] = line

    got("io1l")
    start("io2l+", "io2l-")
    got("scales")
    spread(1)
    text_setup(1)
    image_setup(1)
    got("io1r")
    start("x11", "x1-1", "s2", "s3")
    got("ip")
    start("iq1+", "iq1-", "io2r+", "io2r-", "s1", "t1oNb")
    told(0)
    tell(1)
    got("tp")
    start("t1qP", "t2qP", "t1qNa", "t2qNa")
    got("s0")

    def events(i):
        if i == 1:
            got("iq1")
            start("iq2+", "iq2-")
            got("x1")
            start("s4", "s5")
            got("toN")
            start("t1o2B", "t2o2B")
            got("io2")
            start("x22", "x2-2", "t1qNb", "t2qNb", "io3+", "io3-", "s6", "s7")
            got("toP")
            start("t1o2A", "t2o2A")
            got("s2")
        elif i == 3:
            got("s3")
            told(1)
            tell(2)
        elif i == 4:
            got("iq2")
            start("iq3+", "iq3-")
            got("x2")
            start("s8", "s9")
            got("tqN")
            start("t1q2B", "t2q2B")
            got("tqP")
            start("t1q2A", "t2q2A")
        elif i == 5:
            got("io3")
            start("io4+", "io4-", "s10", "s11", "x33", "x3-3")
        elif i == 6:
            got("s4")
        elif i == 7:
            got("s5")
        elif i == 9:
            got("iq3")
            start("iq4+", "iq4-")
            got("t2")
        elif i == 10:
            got("io4")
            start("x44", "s14")
        elif i == 11:
            got("x3")
            start("s12", "s13")
        elif i == 12:
            told(2)
            send_rows((0, 2, 3, 4, 5))
            got("s6")
        elif i == 13:
            got("iq4", "x4")
            start("s15")
        elif i == 14:
            send_rows((1,))
            got("s7")

    dots(0, dl0, dr0)
    dots(1, dl1, dr1)
    scores(0, dl0, dr0)

    @pl.loop(1, STEPS // 2 - 1)
    def _(i):
        for low, high in ((1, 4), (4, 10), (10, 15)):

            @pl.when((i >= low) & (i < high))
            def _(low=low, high=high):
                for at in range(low, high):
                    if at not in (2, 8):

                        @pl.when(i == at)
                        def _(at=at):
                            events(at)

        dots(2 * i, dl0, dr0)
        scores(2 * i - 1, dl1, dr1)
        dots(2 * i + 1, dl1, dr1)
        scores(2 * i, dl0, dr0)

    dots(STEPS - 2, dl0, dr0)
    scores(STEPS - 3, dl1, dr1)
    send_rows((6,))
    dots(STEPS - 1, dl1, dr1)
    scores(STEPS - 2, dl0, dr0)
    sum_columns(range(12))
    scores(STEPS - 1, dl1, dr1)

    send_rows((7,))

    mine = x * 4 + y
    sum_columns(range(12, 16))

    def col_copy(dx, dy):
        return pltpu.make_async_remote_copy(
            src_ref=col_part.at[dx % 2],
            dst_ref=col_recv.at[mine],
            send_sem=col_sem.at[0],
            recv_sem=col_sem.at[1],
            device_id=device(dx=dx, dy=dy),
            device_id_type=pl.DeviceIdType.MESH,
        )

    plane = [(dx, dy) for dx in range(4) for dy in range(4) if (dx, dy) != (0, 0)]
    for dx, dy in sorted(plane, key=lambda d: -(min(d[0], 4 - d[0]) + min(d[1], 4 - d[1]))):
        col_copy(dx, dy).start()
    col_recv[mine] = col_part[0]
    row_recv[0] = row_part[0]

    all_of(row_recv.at[pl.ds(0, 31)], row_sem.at[1])
    line = row_recv[0]
    for number in range(1, 32):
        line = line + row_recv[number]
    row_out[...] = jnp.where(core == 0, line[:, :64], line[:, 64:])
    all_of(col_recv.at[pl.ds(0, 15)], col_sem.at[1])
    def summed(senders):
        return functools.reduce(lambda s, t: s + t, [col_recv[n] for n in senders])[:, :HALF]

    over_x = [summed([(2 * x_hi + a) * 4 + b for a in range(2) for b in range(4)]) for x_hi in range(2)]
    over_y = [summed([a * 4 + 2 * y_hi + b for a in range(4) for b in range(2)]) for y_hi in range(2)]
    parts = []
    for g in range(8):
        x_hi, yy = g // 4, g % 4
        at = 4 + x_hi * 2 + yy % 2
        parts.append(over_x[x_hi][yy : yy + 1])
        parts.append(over_y[yy // 2][at : at + 1])
    for q in range(4):
        a, b, c, d = parts[4 * q : 4 * q + 4]
        col_out[3 * q : 3 * q + 1, :] = jnp.concatenate([a, b[:, :32]], axis=1)
        col_out[3 * q + 1 : 3 * q + 2, :] = jnp.concatenate([b[:, 32:], c[:, :64]], axis=1)
        col_out[3 * q + 2 : 3 * q + 3, :] = jnp.concatenate([c[:, 64:], d], axis=1)

    all_of(tb.at[:, pl.ds(0, 14 * HALF), :], send_sem.at[0])
    all_of(ib.at[:, pl.ds(0, 31 * 64), :], send_sem.at[1])
    all_of(bc.at[0, 0, pl.ds(0, 72), :], send_sem.at[2])
    all_of(row_recv.at[pl.ds(0, 31)], row_sem.at[0])
    all_of(col_recv.at[pl.ds(0, 15)], col_sem.at[0])


def shards(
    image_learn,
    image_refer,
    text_learn,
    text_refer,
    image_scale_learn,
    image_scale_refer,
    text_scale_learn,
    text_scale_refer,
    pair_index,
):
    offset = math.log(text_scale_learn.shape[0] * lax.axis_size("col"))
    vmem, dma = pltpu.VMEM, pltpu.SemaphoreType.DMA
    in_hbm = pl.BlockSpec(memory_space=pltpu.HBM)
    rows, cols = pl.pallas_call(
        functools.partial(kernel, (1.0 - offset) * LOG2E, (-1.0 - offset) * LOG2E),
        out_shape=[jax.ShapeDtypeStruct((1, 64), F32), jax.ShapeDtypeStruct((12, 128), F32)],
        in_specs=[in_hbm] * 9,
        out_specs=[pl.BlockSpec(memory_space=vmem)] * 2,
        scratch_shapes=[
            vmem((2, 4 * CHUNK, E), jnp.bfloat16),
            vmem((2, 8 * BLOCK, E), jnp.bfloat16),
            vmem((2, 2, 16, 128), F32),
            vmem((2, 16, 128), jnp.int32),
            vmem((2, 2, 12, 128), F32),
            vmem((2, 2, 1536, 128), F32),
            vmem((2, 4 * CHUNK, 128), F32),
            vmem((8, 8, BLOCK), F32),
            vmem((8, 8, BLOCK), jnp.int32),
            pltpu.SMEM((16,), jnp.int32),
            vmem((8, 8, BLOCK), F32),
            vmem((4 * CHUNK, 128), F32),
            vmem((CHUNK, BLOCK), F32),
            vmem((CHUNK, BLOCK), F32),
            vmem((CHUNK, BLOCK), F32),
            vmem((CHUNK, BLOCK), F32),
            vmem((16, 1, 128), F32),
            vmem((32, 1, 128), F32),
            vmem((2, 8, 128), F32),
            vmem((16, 8, 128), F32),
            dma((5,)),
            dma((3,)),
            dma((28,)),
            dma((2,)),
            dma((2,)),
            pltpu.SemaphoreType.REGULAR((3,)),
        ],
        compiler_params=pltpu.CompilerParams(
            collective_id=0, has_side_effects=True, vmem_limit_bytes=VMEM_GRANT
        ),
        cost_estimate=pl.CostEstimate(
            flops=4 * 2048 * 1536 * E, bytes_accessed=2**21, transcendentals=3 * 2048 * 1536
        ),
        name="gather_score",
    )(
        image_learn,
        image_refer,
        text_learn,
        text_refer,
        image_scale_learn.reshape(16, 128),
        image_scale_refer.reshape(16, 128),
        text_scale_learn.reshape(12, 128),
        text_scale_refer.reshape(12, 128),
        pair_index.reshape(16, 128),
    )
    return rows.reshape(64), cols.reshape(1536)


def solution(mesh):
    in_specs = (
        P(("grp", "col"), None),
        P(("grp", "col"), None),
        P("col", "grp", None),
        P("col", "grp", None),
        P("grp"),
        P("grp"),
        P("col"),
        P("col"),
        P("grp"),
    )
    out_specs = (P(("grp", "col")), P("col"))
    return jax.shard_map(shards, mesh=mesh, in_specs=in_specs, out_specs=out_specs, check_vma=False)
```

```python
import functools
import math

import jax
import jax.numpy as jnp
from jax import lax
from jax.experimental import pallas as pl
from jax.experimental.pallas import tpu as pltpu
from jax.sharding import PartitionSpec as P

F32 = jnp.float32
LOG2E = 1.0 / math.log(2.0)
LN2 = math.log(2.0)
SERIES = tuple(2.0 * LOG2E * c for c in (0.99999984, 0.33337989, 0.1979503, 0.17111227))

E = 1152
HALF = 96
CHUNK = 4 * HALF
SPLIT = {1: 1024, 2: 1024, 3: 1024, 4: 896}
BLOCK = 256
PIECE_Z = (0, 0, 1, -1, 1, -1, 2, -2, 2, -2, 3, -3, 3, -3, 4, 4)
PIECE_LANE = (0, 1, 0, 0, 1, 1, 0, 0, 1, 1, 0, 0, 1, 1, 0, 1)
STEPS = 32
VMEM_GRANT = 56539217


def wrap(value, size):
    return lax.rem(value + size, size)


def score(dot_learn, dot_refer, a_learn, a_refer, b_learn, b_refer, paired, c_learn, c_refer):
    u = dot_learn * a_learn * b_learn + c_learn
    w = dot_refer * a_refer * b_refer + c_refer
    p = jnp.exp2(-jnp.abs(u))
    q = jnp.exp2(-jnp.abs(w))
    z = (p - q) * pl.reciprocal((p + q) + 2.0, approx=True)
    s = z * z
    poly = s * SERIES[3] + SERIES[2]
    poly = poly * s + SERIES[1]
    poly = poly * s + SERIES[0]
    d = (jnp.maximum(u, 0.0) - jnp.maximum(w, 0.0)) + z * poly
    return d - jnp.where(paired, u - w, 0.0)


def kernel(
    c_learn,
    c_refer,
    img_l,
    img_r,
    txt_l,
    txt_r,
    isc_l,
    isc_r,
    tsc_l,
    tsc_r,
    pair,
    row_out,
    col_out,
    tb,
    ib,
    isc,
    ipr,
    tsc,
    bc,
    tcol,
    irow,
    iprow,
    base,
    rs,
    cs,
    dl0,
    dr0,
    dl1,
    dr1,
    row_part,
    row_recv,
    col_part,
    col_recv,
    local_sem,
    send_sem,
    recv_sem,
    row_sem,
    col_sem,
    ready,
):
    grp, col = lax.axis_index("grp"), lax.axis_index("col")
    x = lax.div(grp, 4) * 2 + lax.rem(lax.div(col, 2), 2)
    y = lax.rem(grp, 4)
    z = lax.div(col, 4)
    core = lax.rem(col, 2)
    x_odd, y_odd = lax.rem(x, 2), lax.rem(y, 2)
    x_pair, y_pair = x + 1 - 2 * x_odd, y + 1 - 2 * y_odd
    x_diag, y_diag = wrap(x - 1 + 2 * x_odd, 4), wrap(y - 1 + 2 * y_odd, 4)

    def device(dx=0, dy=0, dz=0, at_x=None, at_y=None, at_core=None):
        px = wrap(x + dx, 4) if at_x is None else at_x
        py = wrap(y + dy, 4) if at_y is None else at_y
        pz = wrap(z + dz, 8)
        pc = core if at_core is None else at_core
        return lax.div(px, 2) * 4 + py, (pz * 2 + lax.rem(px, 2)) * 2 + pc

    other_core = device(at_core=1 - core)
    diag = device(at_x=x_diag, at_y=y_diag)
    pair_x, next_x = device(at_x=x_pair), device(at_x=x_diag)
    pair_y, next_y = device(at_y=y_pair), device(at_y=y_diag)
    up_z, dn_z = device(dz=1), device(dz=-1)

    groups, messages = {}, {}

    def group(name, ref):
        groups[name] = (len(groups), ref)

    def message(name, group_name, copies, to):
        messages[name] = (group_name, copies, to)

    def text(piece, start=0, rows=HALF):
        return tb.at[:, pl.ds(piece * HALF + start, rows), :]

    def image(piece, part=None, first=0, size=E):
        rows = 64 if part is None else 32
        off = piece * 128 + core * 64 + (0 if part is None else part * 32)
        return ib.at[:, pl.ds(pl.multiple_of(off, 32), rows), pl.ds(first, size)]

    group("scales", bc.at[0, 0, pl.ds(0, 72), :])
    message("tsc", "scales", [(tsc_l, tsc.at[1, 0]), (tsc_r, tsc.at[1, 1])], pair_x)
    message("isc", "scales", [(isc_l, isc.at[1, 0]), (isc_r, isc.at[1, 1]), (pair, ipr.at[1])], diag)
    group("tp", tb.at[:, pl.ds(0, 192), :])
    first, second = pl.ds(0, HALF), pl.ds(HALF, HALF)
    message("t1p", "tp", [(t.at[0, first, :], text(2).at[i]) for i, t in enumerate((txt_l, txt_r))], pair_x)
    message("t2p", "tp", [(t.at[0, second, :], text(3).at[i]) for i, t in enumerate((txt_l, txt_r))], pair_y)
    group("ip", ib.at[:, pl.ds(0, 64), :])
    message("ip", "ip", [(r, image(1).at[i]) for i, r in enumerate((img_l, img_r))], diag)
    for name in ("oP", "oN", "qP", "qN"):
        group("t" + name, tb.at[:, pl.ds(0, 192), :])
    group("t2", tb.at[:, pl.ds(0, 384), :])
    for name, first, to_p, to_n in (("t1", 0, pair_y, next_y), ("t2", 1, pair_x, next_x)):
        o, far = 4 + 2 * first, 12 + first
        message(name + "oP", "toP", [(text(first), text(o))], to_p)
        for part, start_row, rows in (("a", 0, 64), ("b", 64, 32)):
            message(name + "oN" + part, "toN", [(text(first, start_row, rows), text(o + 1, start_row, rows))], to_n)
        message(name + "qP", "tqP", [(text(2 + first), text(o + 4))], to_p)
        for part, start_row, rows in (("a", 0, 64), ("b", 64, 32)):
            piece = [(text(2 + first, start_row, rows), text(o + 5, start_row, rows))]
            message(name + "qN" + part, "tqN", piece, to_n)
        message(name + "o2A", "t2", [(text(o, 0, 48), text(far, 0, 48))], to_n)
        message(name + "o2B", "t2", [(text(o + 1, 48, 48), text(far, 48, 48))], to_p)
        message(name + "q2A", "t2", [(text(o + 4, 0, 48), text(far + 2, 0, 48))], to_n)
        message(name + "q2B", "t2", [(text(o + 5, 48, 48), text(far + 2, 48, 48))], to_p)
    for lane, mark in ((0, "o"), (1, "q")):
        place = {dz: p for p, dz in enumerate(PIECE_Z) if PIECE_LANE[p] == lane}
        for k in (1, 2, 3, 4):
            size = E if lane == 0 else SPLIT[k]
            ring = f"i{mark}{k}"
            if ring != "io1":
                group(ring, ib.at[:, pl.ds(0, 128 if k < 4 else 64), pl.ds(0, size)])
            if ring in ("io1", "io2"):
                for i, (part, own) in enumerate((("l", img_l), ("r", img_r))):
                    if ring == "io1":
                        group(ring + part, ib.at[0, pl.ds(0, 128), :])
                    for sign, to, at in (("+", dn_z, 1), ("-", up_z, -1)):
                        src = own if ring == "io1" else image(place[at]).at[i]
                        group_name = ring + part if ring == "io1" else ring
                        message(ring + part + sign, group_name, [(src, image(place[k * at]).at[i])], to)
            elif k < 4:
                message(ring + "+", ring, [(image(place[k - 1], size=size), image(place[k], size=size))], dn_z)
                message(ring + "-", ring, [(image(place[1 - k], size=size), image(place[-k], size=size))], up_z)
            else:
                message(ring + "+", ring, [(image(place[3], 0, size=size), image(place[4], 0, size=size))], dn_z)
                message(ring + "-", ring, [(image(place[-3], 1, size=size), image(place[4], 1, size=size))], up_z)
            if lane == 0 and SPLIT[k] < E:
                rest = dict(first=SPLIT[k], size=E - SPLIT[k])
                group(f"x{k}", ib.at[:, pl.ds(0, 128 if k < 4 else 64), pl.ds(0, E - SPLIT[k])])
                for at in (k, -k) if k < 4 else (k,):
                    there = [p for p in range(16) if PIECE_Z[p] == at and PIECE_LANE[p] == 1][0]
                    message(f"x{k}{at}", f"x{k}", [(image(place[at], **rest), image(there, **rest))], diag)
    for block in range(8):
        if block != 1:
            group(f"s{block}", ib.at[:, pl.ds(0, 128 if block else 256), :])
    for piece in range(16):
        message(f"s{piece}", f"s{piece // 2 if piece > 3 else 0}", [(image(piece), image(piece))], other_core)

    def sender(name):
        return 2 if name in ("tsc", "isc") else 0 if name[0] == "t" else 1

    def start(*names):
        for name in names:
            group_name, copies, to = messages[name]
            for src, dst in copies:
                pltpu.make_async_remote_copy(
                    src_ref=src,
                    dst_ref=dst,
                    send_sem=send_sem.at[sender(name)],
                    recv_sem=recv_sem.at[groups[group_name][0]],
                    device_id=to,
                    device_id_type=pl.DeviceIdType.MESH,
                ).start()

    def all_of(ref, sem):
        pltpu.make_async_copy(ref, ref, sem).wait()

    def got(*names):
        for name in names:
            number, ref = groups[name]
            all_of(ref, recv_sem.at[number])

    own_rows = pl.ds(pl.multiple_of(core * 64, 64), 64)
    barrier = pltpu.get_barrier_semaphore()
    near = (pair_x, next_x, pair_y, next_y)
    for to in near + (up_z, dn_z, other_core, diag):
        pl.semaphore_signal(barrier, inc=1, device_id=to, device_id_type=pl.DeviceIdType.MESH)
    loads = [
        (0, txt_l.at[0], tb.at[0, pl.ds(0, 2 * HALF), :]),
        (0, txt_r.at[0], tb.at[1, pl.ds(0, 2 * HALF), :]),
        (1, img_l, ib.at[0, own_rows, :]),
        (1, img_r, ib.at[1, own_rows, :]),
        (2, isc_l, isc.at[0, 0]),
        (2, isc_r, isc.at[0, 1]),
        (3, tsc_l, tsc.at[0, 0]),
        (3, tsc_r, tsc.at[0, 1]),
        (4, pair, ipr.at[0]),
    ]
    for number, src, dst in loads:
        pltpu.make_async_copy(src, dst, local_sem.at[number]).start()

    pl.semaphore_wait(barrier, 8)
    start("tsc", "isc", "ip", "t1p", "t2p", "io1l+", "io1l-", "io1r+", "io1r-")
    for number, ref in enumerate((tb.at[:, pl.ds(0, 2 * HALF), :], ib.at[:, own_rows, :], isc.at[0], tsc.at[0], ipr.at[0])):
        all_of(ref, local_sem.at[number])
    start("s0", "t1oNa", "t2oNa", "t2oNb", "t1oP", "t2oP")

    def tell(r):
        for to in near:
            pl.semaphore_signal(ready.at[r], inc=1, device_id=to, device_id_type=pl.DeviceIdType.MESH)

    def told(r):
        pl.semaphore_wait(ready.at[r], 4)

    tell(0)

    def source(piece):
        if piece < 4:
            lane, half, side = piece // 2, piece % 2, 0
        elif piece < 12:
            lane, half, side = (piece - 4) // 4, ((piece - 4) // 2) % 2, 1 + piece % 2
        else:
            lane, half, side = (piece - 12) // 2, piece % 2, 3
        along_x, along_y = (x, x_pair, x_diag, wrap(x + 2, 4)), (y, y_pair, y_diag, wrap(y + 2, 4))
        px = along_x[side] if half == 1 else along_x[lane]
        py = along_y[side] if half == 0 else along_y[lane]
        same = lane == 0 if half == 0 else side in (0, 3)
        return px, py, half, same

    def spread(which):
        @pl.loop(0, 24)
        def _(i):
            k, q = lax.div(i, 12), lax.rem(i, 12)
            line = tsc[which, k, pl.ds(q, 1), :]
            bc[which, k, pl.ds(pl.multiple_of(q * 128, 128), 128), :] = jnp.transpose(
                jnp.broadcast_to(line, (128, 128))
            )

    def text_setup(which):
        for piece in range(16):
            px, py, half, same = source(piece)
            if same != (which == 0):
                continue
            off = (lax.div(px, 2) * 4 + py) * 192 + half * HALF
            block = (z * 2 + lax.rem(px, 2)) * 2 + core
            base[piece] = block * 1536 + off
            for k in range(2):
                tcol[k, pl.ds(piece * HALF, HALF), :] = bc[which, k, pl.ds(pl.multiple_of(off, 32), HALF), :]

    def image_setup(lane):
        odd = x_odd if lane == 0 else 1 - x_odd
        for piece in range(16):
            if PIECE_LANE[piece] != lane:
                continue
            block, lanes = piece // 2, pl.ds((piece % 2) * 128, 128)
            at = pl.ds(wrap(z + PIECE_Z[piece], 8) * 2 + odd, 1)
            irow[block, 0:1, lanes] = isc[lane, 0, at, :] * (4.0 * LOG2E)
            irow[block, 1:2, lanes] = isc[lane, 1, at, :] * (6.0 * LOG2E)
            iprow[block, 0:1, lanes] = ipr[lane, at, :]

    def tile(k):
        block = jnp.where(
            k < 18,
            jnp.where(
                k < 8,
                jnp.where(k < 6, lax.rem(k, 3), 3),
                jnp.where(k < 12, k - 8, lax.div(k, 3)),
            ),
            jnp.where(k < 24, jnp.where(k < 22, k - 16, k - 22), lax.div(k, 4)),
        )
        chunk = jnp.where(
            k < 18,
            jnp.where(k < 8, jnp.where(k < 6, lax.div(k, 3), k - 6), jnp.where(k < 12, 2, lax.rem(k, 3))),
            jnp.where(k < 24, 3, lax.rem(k, 4)),
        )
        return block, chunk

    def dots(k, dl, dr):
        block, chunk = tile(k)
        rows = pl.ds(pl.multiple_of(chunk * CHUNK, CHUNK), CHUNK)
        cols = pl.ds(pl.multiple_of(block * BLOCK, BLOCK), BLOCK)
        for which, out in ((0, dl), (1, dr)):
            out[...] = lax.dot_general(
                tb[which, rows, :], ib[which, cols, :], (((1,), (1,)), ((), ())), preferred_element_type=F32
            )

    def scores(k, dl, dr):
        block, chunk = tile(k)
        scale = irow[block]
        a_learn = jnp.broadcast_to(scale[0:1], (8, BLOCK))
        a_refer = jnp.broadcast_to(scale[1:2], (8, BLOCK))
        wanted = jnp.broadcast_to(iprow[block][0:1], (8, BLOCK)) - lax.broadcasted_iota(jnp.int32, (8, BLOCK), 0)
        total = rs[block]
        for piece in range(4):
            here = wanted - base[chunk * 4 + piece]
            for g in range(HALF // 8):
                at = piece * HALF + g * 8
                rows = pl.ds(pl.multiple_of(chunk * CHUNK + at, 8), 8)
                b_learn, b_refer = tcol[0, rows, :], tcol[1, rows, :]
                d = score(
                    dl[at : at + 8, :],
                    dr[at : at + 8, :],
                    a_learn,
                    a_refer,
                    jnp.concatenate([b_learn, b_learn], axis=1),
                    jnp.concatenate([b_refer, b_refer], axis=1),
                    here == g * 8,
                    c_learn,
                    c_refer,
                )
                total = total + d
                cs[rows, :] = cs[rows, :] + (d[:, :128] + d[:, 128:])
        rs[block] = total

    rs[...] = jnp.zeros_like(rs)
    cs[...] = jnp.zeros_like(cs)
    spread(0)
    text_setup(0)
    image_setup(0)

    def row_copy(piece, which):
        number = piece * 2 + which
        at_core = core if which == 0 else 1 - core
        if PIECE_LANE[piece] == 0:
            to = device(dz=PIECE_Z[piece], at_core=at_core)
        else:
            to = device(dz=PIECE_Z[piece], at_x=x_diag, at_y=y_diag, at_core=at_core)
        return pltpu.make_async_remote_copy(
            src_ref=row_part.at[piece],
            dst_ref=row_recv.at[number],
            send_sem=row_sem.at[0],
            recv_sem=row_sem.at[1],
            device_id=to,
            device_id_type=pl.DeviceIdType.MESH,
        )

    row_messages = [(piece, which) for piece in range(16) for which in range(2) if (piece, which) != (0, 0)]

    def send_rows(blocks):
        for block in blocks:
            line = jnp.sum(rs[block], axis=0, keepdims=True) * LN2
            row_part[block * 2] = line[:, :128]
            row_part[block * 2 + 1] = line[:, 128:]
        for piece, which in reversed(row_messages):
            if piece // 2 in blocks:
                row_copy(piece, which).start()

    def sum_columns(pieces):
        for piece in pieces:
            px, py, half, same = source(piece)
            line = jnp.sum(jnp.transpose(cs[pl.ds(piece * HALF, HALF), :]), axis=0, keepdims=True) * LN2
            place = py if half == 0 else 4 + lax.div(px, 2) * 2 + lax.rem(py, 2)
            col_part[0 if same else 1, pl.ds(place, 1), 0:HALF] = line

    got("io1l")
    start("io2l+", "io2l-")
    got("scales")
    spread(1)
    text_setup(1)
    image_setup(1)
    got("io1r")
    start("x11", "x1-1", "s2", "s3")
    got("ip")
    start("iq1+", "iq1-", "io2r+", "io2r-", "s1", "t1oNb")
    told(0)
    tell(1)
    got("tp")
    start("t1qP", "t2qP", "t1qNa", "t2qNa")
    got("s0")

    def events(i):
        if i == 1:
            got("iq1")
            start("iq2+", "iq2-")
            got("x1")
            start("s4", "s5")
            got("toN")
            start("t1o2B", "t2o2B")
            got("io2")
            start("x22", "x2-2", "t1qNb", "t2qNb", "io3+", "io3-", "s6", "s7")
            got("toP")
            start("t1o2A", "t2o2A")
            got("s2")
        elif i == 3:
            got("s3")
            told(1)
            tell(2)
        elif i == 4:
            got("iq2")
            start("iq3+", "iq3-")
            got("x2")
            start("s8", "s9")
            got("tqN")
            start("t1q2B", "t2q2B")
            got("tqP")
            start("t1q2A", "t2q2A")
        elif i == 5:
            got("io3")
            start("io4+", "io4-", "s10", "s11", "x33", "x3-3")
        elif i == 6:
            got("s4")
        elif i == 7:
            got("s5")
        elif i == 9:
            got("iq3")
            start("iq4+", "iq4-")
            got("t2")
        elif i == 10:
            got("io4")
            start("x44", "s14")
        elif i == 11:
            got("x3")
            start("s12", "s13")
        elif i == 12:
            told(2)
            send_rows((0, 2, 3, 4, 5))
            got("s6")
        elif i == 13:
            got("iq4", "x4")
            start("s15")
        elif i == 14:
            send_rows((1,))
            got("s7")

    dots(0, dl0, dr0)
    dots(1, dl1, dr1)
    scores(0, dl0, dr0)

    @pl.loop(1, STEPS // 2 - 1)
    def _(i):
        for low, high in ((1, 4), (4, 10), (10, 15)):

            @pl.when((i >= low) & (i < high))
            def _(low=low, high=high):
                for at in range(low, high):
                    if at not in (2, 8):

                        @pl.when(i == at)
                        def _(at=at):
                            events(at)

        dots(2 * i, dl0, dr0)
        scores(2 * i - 1, dl1, dr1)
        dots(2 * i + 1, dl1, dr1)
        scores(2 * i, dl0, dr0)

    dots(STEPS - 2, dl0, dr0)
    scores(STEPS - 3, dl1, dr1)
    send_rows((6,))
    dots(STEPS - 1, dl1, dr1)
    scores(STEPS - 2, dl0, dr0)
    sum_columns(range(12))
    scores(STEPS - 1, dl1, dr1)

    send_rows((7,))

    mine = x * 4 + y
    sum_columns(range(12, 16))

    def col_copy(dx, dy):
        return pltpu.make_async_remote_copy(
            src_ref=col_part.at[dx % 2],
            dst_ref=col_recv.at[mine],
            send_sem=col_sem.at[0],
            recv_sem=col_sem.at[1],
            device_id=device(dx=dx, dy=dy),
            device_id_type=pl.DeviceIdType.MESH,
        )

    plane = [(dx, dy) for dx in range(4) for dy in range(4) if (dx, dy) != (0, 0)]
    for dx, dy in sorted(plane, key=lambda d: -(min(d[0], 4 - d[0]) + min(d[1], 4 - d[1]))):
        col_copy(dx, dy).start()
    col_recv[mine] = col_part[0]
    row_recv[0] = row_part[0]

    all_of(row_recv.at[pl.ds(0, 31)], row_sem.at[1])
    line = row_recv[0]
    for number in range(1, 32):
        line = line + row_recv[number]
    row_out[...] = jnp.where(core == 0, line[:, :64], line[:, 64:])
    all_of(col_recv.at[pl.ds(0, 15)], col_sem.at[1])
    def summed(senders):
        return functools.reduce(lambda s, t: s + t, [col_recv[n] for n in senders])[:, :HALF]

    over_x = [summed([(2 * x_hi + a) * 4 + b for a in range(2) for b in range(4)]) for x_hi in range(2)]
    over_y = [summed([a * 4 + 2 * y_hi + b for a in range(4) for b in range(2)]) for y_hi in range(2)]
    parts = []
    for g in range(8):
        x_hi, yy = g // 4, g % 4
        at = 4 + x_hi * 2 + yy % 2
        parts.append(over_x[x_hi][yy : yy + 1])
        parts.append(over_y[yy // 2][at : at + 1])
    for q in range(4):
        a, b, c, d = parts[4 * q : 4 * q + 4]
        col_out[3 * q : 3 * q + 1, :] = jnp.concatenate([a, b[:, :32]], axis=1)
        col_out[3 * q + 1 : 3 * q + 2, :] = jnp.concatenate([b[:, 32:], c[:, :64]], axis=1)
        col_out[3 * q + 2 : 3 * q + 3, :] = jnp.concatenate([c[:, 64:], d], axis=1)

    all_of(tb.at[:, pl.ds(0, 14 * HALF), :], send_sem.at[0])
    all_of(ib.at[:, pl.ds(0, 31 * 64), :], send_sem.at[1])
    all_of(bc.at[0, 0, pl.ds(0, 72), :], send_sem.at[2])
    all_of(row_recv.at[pl.ds(0, 31)], row_sem.at[0])
    all_of(col_recv.at[pl.ds(0, 15)], col_sem.at[0])


def shards(
    image_learn,
    image_refer,
    text_learn,
    text_refer,
    image_scale_learn,
    image_scale_refer,
    text_scale_learn,
    text_scale_refer,
    pair_index,
):
    offset = math.log(text_scale_learn.shape[0] * lax.axis_size("col"))
    vmem, dma = pltpu.VMEM, pltpu.SemaphoreType.DMA
    in_hbm = pl.BlockSpec(memory_space=pltpu.HBM)
    rows, cols = pl.pallas_call(
        functools.partial(kernel, (1.0 - offset) * LOG2E, (-1.0 - offset) * LOG2E),
        out_shape=[jax.ShapeDtypeStruct((1, 64), F32), jax.ShapeDtypeStruct((12, 128), F32)],
        in_specs=[in_hbm] * 9,
        out_specs=[pl.BlockSpec(memory_space=vmem)] * 2,
        scratch_shapes=[
            vmem((2, 4 * CHUNK, E), jnp.bfloat16),
            vmem((2, 8 * BLOCK, E), jnp.bfloat16),
            vmem((2, 2, 16, 128), F32),
            vmem((2, 16, 128), jnp.int32),
            vmem((2, 2, 12, 128), F32),
            vmem((2, 2, 1536, 128), F32),
            vmem((2, 4 * CHUNK, 128), F32),
            vmem((8, 8, BLOCK), F32),
            vmem((8, 8, BLOCK), jnp.int32),
            pltpu.SMEM((16,), jnp.int32),
            vmem((8, 8, BLOCK), F32),
            vmem((4 * CHUNK, 128), F32),
            vmem((CHUNK, BLOCK), F32),
            vmem((CHUNK, BLOCK), F32),
            vmem((CHUNK, BLOCK), F32),
            vmem((CHUNK, BLOCK), F32),
            vmem((16, 1, 128), F32),
            vmem((32, 1, 128), F32),
            vmem((2, 8, 128), F32),
            vmem((16, 8, 128), F32),
            dma((5,)),
            dma((3,)),
            dma((28,)),
            dma((2,)),
            dma((2,)),
            pltpu.SemaphoreType.REGULAR((3,)),
        ],
        compiler_params=pltpu.CompilerParams(
            collective_id=0, has_side_effects=True, vmem_limit_bytes=VMEM_GRANT
        ),
        cost_estimate=pl.CostEstimate(
            flops=4 * 2048 * 1536 * E, bytes_accessed=2**21, transcendentals=3 * 2048 * 1536
        ),
        name="gather_score",
    )(
        image_learn,
        image_refer,
        text_learn,
        text_refer,
        image_scale_learn.reshape(16, 128),
        image_scale_refer.reshape(16, 128),
        text_scale_learn.reshape(12, 128),
        text_scale_refer.reshape(12, 128),
        pair_index.reshape(16, 128),
    )
    return rows.reshape(64), cols.reshape(1536)


def solution(mesh):
    in_specs = (
        P(("grp", "col"), None),
        P(("grp", "col"), None),
        P("col", "grp", None),
        P("col", "grp", None),
        P("grp"),
        P("grp"),
        P("col"),
        P("col"),
        P("grp"),
    )
    out_specs = (P(("grp", "col")), P("col"))
    return jax.shard_map(shards, mesh=mesh, in_specs=in_specs, out_specs=out_specs, check_vma=False)
```
